256 devices in a mesh: mem: 16 (over y_hi, x, core), sp: 16 (over z, y_lo).
Axes of the slice: x: 4, y: 4 (y_hi: 2, y_lo: 2; y = y_hi * 2 + y_lo), z: 8, core: 2. Of those that a mesh axis runs over, the one named last changes fastest.
Arguments:
- background_samples: bfloat16 [1024, 65536], P('mem', 'sp'), may hold values from -8 to 8
- sensor_cell_offsets: int32 [131072], P('sp'), may hold values from 0 to 4095
- sensor_data: float32 [131072], P('sp'), may hold values from -6 to 6
- sensor_sigma_list: float32 [131072], P('sp'), may hold values from 1.5 to 2.5
Outputs:
- analysis: bfloat16 [1024, 65536], P('mem', 'sp')
The draws below stay inside these ranges and needn't reach their ends.
Inputs may be any that keep to these rules, and one draw needn't show every extreme that they name: Observation j reads state row (j // 8192) * 4096 + sensor_cell_offsets[j].
All inputs are finite; a program needn't handle non-finite values.
Results may differ from the reference program's by a relative error of at most 0.0064.
Values may be sent and summed in bfloat16 or wider, within the bound.
No kernel may reach another device: no remote copies, remote signals or barrier semaphores. Data moves between devices by JAX's collectives and lax.ppermute only.
A program may use at most 128 MiB of HBM per device.

```python
import math
import jax
import jax.numpy as jnp
from jax import lax

TRIAL_NUMBER = 1024
ROWS_DEV = 4096
OBS_DEV = 8192
NSTATE = 65536
NOBS = 131072


def draw_background_samples(key, part):
    key = jax.random.fold_in(key, 17)
    subkeys = jax.random.split(key, 4)
    row_mean = 0.5 * jax.random.normal(subkeys[0], (1, NSTATE), jnp.float32)
    member_trend = 1.0 + 2.0 * jnp.arange(TRIAL_NUMBER, dtype=jnp.float32) / (TRIAL_NUMBER - 1)
    col_scale = jnp.exp(jax.random.uniform(subkeys[1], (TRIAL_NUMBER, 1), jnp.float32, math.log(0.5), math.log(2.0))) * member_trend[:, None]
    row_scale = jnp.exp(jax.random.uniform(subkeys[2], (1, NSTATE), jnp.float32, math.log(0.3), math.log(0.5)))
    member_noise = jax.random.normal(subkeys[3], (TRIAL_NUMBER + 3, NSTATE), jnp.float32)
    noise_part = 0.5 * (member_noise[3:] + member_noise[2:-1] + member_noise[1:-2] + member_noise[:-3])
    values = row_mean + row_scale * col_scale * noise_part
    return jnp.clip(values, -8.0, 8.0).astype(jnp.bfloat16)


def set_ends(entries, stream_key, least, high):
    place = [jax.random.randint(jax.random.fold_in(stream_key, axis), (), 0, length) for axis, length in enumerate(entries.shape)]
    main_axis = entries.shape.index(max(entries.shape))
    neighbour = place[:main_axis] + [(place[main_axis] + 1) % entries.shape[main_axis]] + place[main_axis + 1:]
    return entries.at[tuple(place)].set(least).at[tuple(neighbour)].set(high)


def block_scale(rng, dims, cuts, smallest, top_value):
    def one(axis_at, shards_of):
        draws = jax.random.uniform(jax.random.fold_in(jax.random.fold_in(rng, 6), axis_at), (shards_of,), jnp.float32, smallest / len(cuts), top_value / len(cuts))
        return jnp.repeat(jnp.exp(draws), dims[axis_at] // shards_of).reshape((-1,) + (1,) * (len(dims) - axis_at - 1))

    level = one(*cuts[0])
    for cut in cuts[1:]:
        level = level * one(*cut)
    return level


def centred(rng, shape, scale, bound, shards=(), kind=jnp.bfloat16):
    level = block_scale(rng, shape, shards, -0.22, 0.18) if shards else 1.0
    result = jax.random.normal(rng, shape, jnp.float32) * scale * level
    return jnp.minimum(jnp.maximum(result, -bound), bound).astype(kind)


def setup_inputs(seed: int = 0) -> dict:
    splits = jax.random.split(jax.random.key(seed), 5)
    background_samples = draw_background_samples(jax.random.fold_in(splits[4], 71), 0)
    sensor_cell_offsets = set_ends(jax.random.randint(splits[1], (NOBS,), 0, ROWS_DEV), jax.random.fold_in(splits[1], 1), 0, ROWS_DEV - 1).astype(jnp.int32)
    sensor_data = centred(splits[2], (NOBS,), 1.5, 6.0, ((0, 16),), jnp.float32)
    sensor_sigma_list = jnp.clip(jnp.exp(math.log(2.5) - 0.51082562 * jax.random.uniform(splits[3], (NOBS,), jnp.float32) ** block_scale(splits[3], (NOBS,), ((0, 16),), -0.2, 0.2)), 1.5, 2.5)
    return dict(background_samples=background_samples, sensor_cell_offsets=sensor_cell_offsets, sensor_data=sensor_data, sensor_sigma_list=sensor_sigma_list)


def reference(background_samples, sensor_cell_offsets, sensor_data, sensor_sigma_list):
    predicted_centroid = lax.optimization_barrier(jnp.sum(background_samples, axis=0, dtype=jnp.float32)) / TRIAL_NUMBER
    centred_spread_matrix = (background_samples.astype(jnp.float32) - predicted_centroid[None, :]).astype(jnp.bfloat16)
    block_start = jnp.arange(NOBS, dtype=jnp.int32) // OBS_DEV * ROWS_DEV
    model_lines = (block_start + sensor_cell_offsets).astype(jnp.int32)
    picked = jnp.take(centred_spread_matrix, model_lines, axis=1)
    scaled = (picked.astype(jnp.float32) / sensor_sigma_list[None, :]).astype(jnp.bfloat16)
    misfit_residual = (sensor_data - jnp.take(predicted_centroid, model_lines)) / sensor_sigma_list
    gram_matrix = jnp.dot(scaled.astype(jnp.float32), scaled.T.astype(jnp.float32), preferred_element_type=jnp.float32)
    gram_matrix = gram_matrix + (TRIAL_NUMBER - 1) * jnp.eye(TRIAL_NUMBER, dtype=jnp.float32)
    obs_drive = jnp.dot(scaled.astype(jnp.float32), misfit_residual, precision=lax.Precision.HIGHEST)
    factor = jnp.linalg.cholesky(gram_matrix)
    mean_weights = jax.scipy.linalg.cho_solve((factor, True), obs_drive)
    root_full = jax.scipy.linalg.solve_triangular(factor, jnp.eye(TRIAL_NUMBER, dtype=jnp.float32), trans=1, lower=True)
    root_full = root_full * math.sqrt(TRIAL_NUMBER - 1)
    transform = (root_full + mean_weights[:, None]).astype(jnp.bfloat16)
    multiplied_result = jnp.dot(transform.T.astype(jnp.float32), centred_spread_matrix.astype(jnp.float32), preferred_element_type=jnp.float32)
    return (predicted_centroid[None, :] + multiplied_result).astype(jnp.bfloat16)
```

```python
import math

import jax
import jax.numpy as jnp
from jax import lax
from jax.experimental import pallas as pl
from jax.experimental.pallas import tpu as pltpu
from jax.sharding import Mesh, PartitionSpec as P

F32 = jnp.float32
BF = jnp.bfloat16
N = 1024
CELLS = 4096
OBS = 8192
HALF = CELLS // 2
NB = 128
SB = 8
NK = N // NB
NT = 5
ROWS = 384
DRIVE = NT * 64
VMEM = pl.BlockSpec(memory_space=pltpu.VMEM)
SMEM = pl.BlockSpec(memory_space=pltpu.SMEM)
NTDOT = (((1,), (1,)), ((), ()))
TNDOT = (((0,), (0,)), ((), ()))


def params(mib):
    return pltpu.CompilerParams(vmem_limit_bytes=mib * 2**20)


def split3(x):
    h = x.astype(BF)
    r = x - h.astype(F32)
    m = r.astype(BF)
    return h, m, (r - m.astype(F32)).astype(BF)


def at(i, size):
    return pl.ds(pl.multiple_of(i * size, size), size)


def obs_kernel(scal, off_ref, data_ref, sigma_ref, out_ref, lhs, oh):
    core = scal[2]
    hi_iota = lax.broadcasted_iota(jnp.int32, (16, NB), 0) + core * 16
    lo_iota = lax.broadcasted_iota(jnp.int32, (NB, NB), 0)
    for r in range(OBS // NB):
        off = off_ref[r : r + 1, :]
        sigma = sigma_ref[r : r + 1, :]
        w = 1.0 / (sigma * sigma)
        s = data_ref[r : r + 1, :] * w
        mask = lax.shift_right_logical(off, 7) == hi_iota
        cols = slice(r * NB, (r + 1) * NB)
        for i, v in enumerate(split3(w) + split3(s)):
            v = jnp.broadcast_to(v.astype(F32), (16, NB))
            lhs[16 * i : 16 * i + 16, cols] = jnp.where(mask, v, 0.0).astype(BF)
        oh[:, cols] = jnp.where((off & 127) == lo_iota, 1.0, 0.0).astype(BF)
    t = lax.dot_general(lhs[...], oh[...], NTDOT, preferred_element_type=F32)
    w = t[0:16] + t[16:32] + t[32:48]
    s = t[48:64] + t[64:80] + t[80:96]
    out_ref[...] = jnp.zeros_like(out_ref)
    for h in range(16):
        out_ref[0:1, h * NB : (h + 1) * NB] = w[h : h + 1]
        out_ref[1:2, h * NB : (h + 1) * NB] = s[h : h + 1]


def obs_sums(scal, off, data, sigma):
    shape = (OBS // NB, NB)
    return pl.pallas_call(
        obs_kernel,
        out_shape=jax.ShapeDtypeStruct((8, HALF), F32),
        in_specs=[SMEM, VMEM, VMEM, VMEM],
        out_specs=VMEM,
        scratch_shapes=[pltpu.VMEM((96, OBS), BF), pltpu.VMEM((NB, OBS), BF)],
        compiler_params=params(24),
        cost_estimate=pl.CostEstimate(flops=2 * 96 * NB * OBS, bytes_accessed=200000, transcendentals=0),
        name="obs_sums",
    )(scal, off.reshape(shape), data.reshape(shape), sigma.reshape(shape))


SHIFTS = [(sx, sy) for sy in range(2) for sx in range(4)]


def chip_of(scal, sx, sy):
    return ((scal[0] - sy + 2) % 2) * 4 + (scal[1] - sx + 4) % 4


def gram_kernel(scal, ws_ref, *refs):
    pieces = refs[:8]
    keep, send, mean_ref, b = refs[8:]
    core = scal[2]
    me = scal[0] * 4 + scal[1]
    width = 256

    def cols_body(c, carry):
        cols = at(c, width)
        total = jnp.zeros((1, width), F32)
        for p in pieces:
            total = total + jnp.sum(p[:, cols].astype(F32), axis=0, keepdims=True)
        mean = total * (1.0 / N)
        mean_ref[:, cols] = jnp.broadcast_to(mean, (8, width))
        root = jnp.sqrt(ws_ref[0:1, cols])
        for p, (sx, sy) in zip(pieces, SHIFTS):
            b[at(chip_of(scal, sx, sy), NB), cols] = ((p[:, cols].astype(F32) - mean) * root).astype(BF)
        return carry

    lax.fori_loop(0, HALF // width, cols_body, 0)
    w = ws_ref[0:1, :]
    d = jnp.where(w > 0.0, (ws_ref[1:2, :] - mean_ref[0:1, :] * w) * lax.rsqrt(jnp.where(w > 0.0, w, 1.0)), 0.0)
    d = jnp.concatenate([x.astype(F32) for x in split3(d)] + [jnp.zeros((13, HALF), F32)], axis=0).astype(BF)
    mine = b[at(2 * me + core, 64), :]
    other = b[at(2 * me + 1 - core, 64), :]
    lhs = jnp.concatenate([mine, other], axis=0)
    for i in range(NT):
        rhs = b[at((me + i) % NK, NB), :]
        g = lax.dot_general(lhs, rhs, NTDOT, preferred_element_type=F32)
        keep[64 * i : 64 * i + 64, :] = g[:64]
        send[64 * i : 64 * i + 64, :] = g[64:]
        if i == 0:
            drive = lax.dot_general(d, rhs, NTDOT, preferred_element_type=F32)
            drive = jnp.broadcast_to(jnp.sum(drive, axis=0, keepdims=True), (8, NB))
            for out in (keep, send):
                out[DRIVE : DRIVE + 8, :] = drive
                out[DRIVE + 8 :, :] = jnp.zeros((ROWS - DRIVE - 8, NB), F32)


def gram_part(scal, ws, pieces):
    part = jax.ShapeDtypeStruct((ROWS, NB), F32)
    return pl.pallas_call(
        gram_kernel,
        out_shape=(part, part, jax.ShapeDtypeStruct((8, HALF), F32)),
        in_specs=[SMEM] + [VMEM] * 9,
        out_specs=(VMEM, VMEM, VMEM),
        scratch_shapes=[pltpu.VMEM((N, HALF), BF)],
        compiler_params=params(32),
        cost_estimate=pl.CostEstimate(flops=2 * NB * NB * NT * HALF, bytes_accessed=5 * 2**20, transcendentals=0),
        name="gram_part",
    )(scal, ws, *pieces)


def diag_inverse(dz, vout):
    for j in range(NB // SB):
        r0 = j * SB
        rs = [jnp.broadcast_to(dz[r0 + p : r0 + p + 1, 0:NB], (SB, NB)) for p in range(SB)]
        rw = [jnp.broadcast_to(dz[r0 + p : r0 + p + 1, NB : 2 * NB], (SB, NB)) for p in range(SB)]
        e = [[jnp.broadcast_to(rs[q][:, r0 + p : r0 + p + 1], (SB, NB)) for p in range(q + 1)] for q in range(SB)]
        groups = range(j + 1, NB // SB)
        c = {}
        for g in groups:
            blk = dz[g * SB : (g + 1) * SB, 0:NB]
            c[g] = [jnp.broadcast_to(blk[:, r0 + p : r0 + p + 1], (SB, NB)) for p in range(SB)]
        for p in range(SB):
            r = lax.rsqrt(e[p][p])
            rs[p] = rs[p] * r
            rw[p] = rw[p] * r
            f = {q: e[q][p] * r for q in range(p + 1, SB)}
            for q in range(p + 1, SB):
                for s in range(p + 1, q + 1):
                    e[q][s] = e[q][s] - f[q] * f[s]
            for q in range(p + 1, SB):
                rs[q] = rs[q] - f[q] * rs[p]
                rw[q] = rw[q] - f[q] * rw[p]
            for g in groups:
                c[g][p] = c[g][p] * r
                for q in range(p + 1, SB):
                    c[g][q] = c[g][q] - f[q] * c[g][p]
        for p in range(SB):
            vout[r0 + p : r0 + p + 1, :] = rw[p][0:1, :]
        for g in groups:
            ds = dz[g * SB : (g + 1) * SB, 0:NB]
            dw = dz[g * SB : (g + 1) * SB, NB : 2 * NB]
            for p in range(SB):
                ds = ds - c[g][p] * rs[p]
                dw = dw - c[g][p] * rw[p]
            dz[g * SB : (g + 1) * SB, 0:NB] = ds
            dz[g * SB : (g + 1) * SB, NB : 2 * NB] = dw


def inverse_factor(z, dz, vb, lhs, rhs):
    rows = lax.broadcasted_iota(jnp.int32, (NB, NB), 0)
    eye = jnp.where(rows == lax.broadcasted_iota(jnp.int32, (NB, NB), 1), 1.0, 0.0)
    zero = jnp.zeros((NB, NB), F32)

    def step(k, carry):
        ks = at(k, NB)
        dz[:, 0:NB] = z[ks, ks]
        dz[:, NB : 2 * NB] = eye
        diag_inverse(dz, vb)
        v = vb[...]
        vh, vm, vl = split3(v)
        zh, zm, zl = split3(z[ks, :])
        a = jnp.concatenate([vh, vh, vm, vh, vl, vm], axis=1)
        b = jnp.concatenate([zh, zm, zh, zl, zh, zm], axis=0)
        z[ks, :] = jnp.dot(a, b, preferred_element_type=F32)
        z[ks, ks] = v
        rh, rm, rl = split3(z[ks, :])
        for i, x in enumerate([rh, rm, rh, rl, rh, rm]):
            rhs[i * NB : (i + 1) * NB, :] = x
        for i, x in enumerate([rh, rh, rm, rh, rl, rm]):
            lhs[i * NB : (i + 1) * NB, :] = x

        def trail(i, carry):
            si = at(i, NB)
            z[si, ks] = zero
            z[si, :] = z[si, :] - lax.dot_general(lhs[:, si], rhs[...], TNDOT, preferred_element_type=F32)
            z[ks, si] = zero
            return carry

        return lax.fori_loop(k + 1, NK, trail, carry)

    lax.fori_loop(0, NK, step, 0)


def transform_kernel(scal, ga, gb, t_ref, corr_ref, z, dz, vb, lhs, rhs):
    core = scal[2]
    me = scal[0] * 4 + scal[1]
    rows = lax.broadcasted_iota(jnp.int32, (NB, NB), 0)
    ridge = jnp.where(rows == lax.broadcasted_iota(jnp.int32, (NB, NB), 1), N - 1.0, 0.0)
    half = (lax.broadcasted_iota(jnp.int32, (64, NB), 0) * 0 + core) == 0
    for i in range(NK):
        for d in range(NT):
            j = i + d
            if d == 4 and i >= 4:
                continue
            a = ga[i, 64 * d : 64 * d + 64, :]
            b = gb[i, 64 * d : 64 * d + 64, :]
            blk = jnp.concatenate([jnp.where(half, a, b), jnp.where(half, b, a)], axis=0)
            if d == 0:
                z[i * NB : (i + 1) * NB, i * NB : (i + 1) * NB] = blk + ridge
            elif j < NK:
                z[i * NB : (i + 1) * NB, j * NB : (j + 1) * NB] = blk
            else:
                z[(j - NK) * NB : (j - NK + 1) * NB, i * NB : (i + 1) * NB] = blk.T
    inverse_factor(z, dz, vb, lhs, rhs)
    drive = jnp.concatenate([ga[i, DRIVE : DRIVE + 1, :] for i in range(NK)], axis=1)

    def weigh(i, acc):
        x = z[at(i, 64), :]
        x = x * jnp.sum(x * drive, axis=1, keepdims=True)
        for q in range(8):
            acc = acc + x[q * 8 : (q + 1) * 8]
        return acc

    weights = jnp.sum(lax.fori_loop(0, N // 64, weigh, jnp.zeros((8, N), F32)), axis=0, keepdims=True)
    own = jnp.concatenate([z[at(2 * me + core, 64), :], z[at(2 * me + 1 - core, 64), :]], axis=0)
    t = (own * math.sqrt(N - 1) + weights).astype(BF)
    t_ref[...] = t
    corr_ref[...] = jnp.broadcast_to(1.0 - jnp.sum(t.astype(F32), axis=1, keepdims=True), corr_ref.shape)


def transform(scal, ga, gb):
    return pl.pallas_call(
        transform_kernel,
        out_shape=(jax.ShapeDtypeStruct((NB, N), BF), jax.ShapeDtypeStruct((NB, NB), F32)),
        in_specs=[SMEM, VMEM, VMEM],
        out_specs=(VMEM, VMEM),
        scratch_shapes=[
            pltpu.VMEM((N, N), F32),
            pltpu.VMEM((NB, 2 * NB), F32),
            pltpu.VMEM((NB, NB), F32),
            pltpu.VMEM((6 * NB, N), BF),
            pltpu.VMEM((6 * NB, N), BF),
        ],
        compiler_params=params(40),
        cost_estimate=pl.CostEstimate(flops=10**10, bytes_accessed=4 * 2**20, transcendentals=0),
        name="transform",
    )(scal, ga, gb)


def update_kernel(scal, t_ref, corr_ref, mean_ref, *refs):
    pieces = refs[:8]
    keep, send = refs[8:]
    corr = corr_ref[:, 0:1]
    acc = corr * mean_ref[0:1, :]
    for p, (sx, sy) in zip(pieces, SHIFTS):
        acc = acc + jnp.dot(t_ref[:, at(chip_of(scal, sx, sy), NB)], p[...], preferred_element_type=F32)
    keep[...] = acc[:64].astype(BF)
    send[...] = acc[64:].astype(BF)


def update(scal, t, corr, mean, pieces):
    part = jax.ShapeDtypeStruct((64, HALF), BF)
    return pl.pallas_call(
        update_kernel,
        out_shape=(part, part),
        in_specs=[SMEM] + [VMEM] * 11,
        out_specs=(VMEM, VMEM),
        compiler_params=params(32),
        cost_estimate=pl.CostEstimate(flops=2 * NB * N * HALF, bytes_accessed=5 * 2**20, transcendentals=0),
        name="update",
    )(scal, t, corr, mean, *pieces)


def swap(x):
    return lax.ppermute(x, "core", [(0, 1), (1, 0)])


def from_chip(x, sx, sy):
    if sx + sy == 0:
        return x
    pairs = [(y * 4 + i, ((y + sy) % 2) * 4 + (i + sx) % 4) for y in range(2) for i in range(4)]
    return lax.ppermute(x, ("yh", "x"), pairs)


def gather(x, axes, size):
    return lax.all_to_all(jnp.broadcast_to(x[None], (size, *x.shape)), axes, 0, 0, tiled=True)


def per_device(background_samples, sensor_cell_offsets, sensor_data, sensor_sigma_list):
    core = lax.axis_index("core")
    scal = jnp.stack([lax.axis_index("yh"), lax.axis_index("x"), core]).astype(jnp.int32)
    low, high = background_samples[:, :HALF], background_samples[:, HALF:]
    first = core == 0
    mine = jnp.where(first, low, high)
    got = swap(jnp.where(first, high, low))
    block = jnp.where(first, jnp.concatenate([mine, got]), jnp.concatenate([got, mine]))
    pieces = [from_chip(block, sx, sy) for sx, sy in SHIFTS]
    ws = obs_sums(scal, sensor_cell_offsets, sensor_data, sensor_sigma_list)
    keep, send, mean = gram_part(scal, ws, pieces)
    part = keep + swap(send)
    part = lax.all_to_all(part.reshape(16, 24, NB), ("z", "yl"), 0, 0, tiled=True)
    part = gather(jnp.sum(part, axis=0), ("z", "yl"), 16).reshape(ROWS, NB)
    ga = gather(part, ("yh", "x"), 8)
    gb = swap(ga)
    t, corr = transform(scal, ga, gb)
    keep, send = update(scal, t, corr, mean, pieces)
    got = swap(send)
    return jnp.where(first, jnp.concatenate([keep, got], axis=1), jnp.concatenate([got, keep], axis=1))


def solution(mesh):
    names = ("yh", "x", "core", "z", "yl")
    split = Mesh(mesh.devices.reshape(2, 4, 2, 8, 2), names)
    mem, sp = names[:3], names[3:]
    return jax.shard_map(
        per_device,
        mesh=split,
        in_specs=(P(mem, sp), P(sp), P(sp), P(sp)),
        out_specs=P(mem, sp),
        check_vma=False,
    )
```

```python
import math

import jax
import jax.numpy as jnp
from jax import lax
from jax.experimental import pallas as pl
from jax.experimental.pallas import tpu as pltpu
from jax.sharding import Mesh, PartitionSpec as P

F32 = jnp.float32
BF = jnp.bfloat16
N = 1024
CELLS = 4096
OBS = 8192
HALF = CELLS // 2
NB = 128
SB = 8
NK = N // NB
PART = CELLS // NK
PART_HI = PART // NB
GROWS = 144
VMEM = pl.BlockSpec(memory_space=pltpu.VMEM)
SMEM = pl.BlockSpec(memory_space=pltpu.SMEM)
NTDOT = (((1,), (1,)), ((), ()))
TNDOT = (((0,), (0,)), ((), ()))


def params(mib):
    return pltpu.CompilerParams(vmem_limit_bytes=mib * 2**20)


def split3(x):
    h = x.astype(BF)
    r = x - h.astype(F32)
    m = r.astype(BF)
    return h, m, (r - m.astype(F32)).astype(BF)


def at(i, size):
    return pl.ds(pl.multiple_of(i * size, size), size)


def obs_kernel(scal, off_ref, data_ref, sigma_ref, out_ref, lhs, oh):
    first = (scal[0] * 4 + scal[1]) * PART_HI
    row = lax.broadcasted_iota(jnp.int32, (8, NB), 0)
    hi_iota = (row & 3) + first
    lower = row < 4
    lo_iota = lax.broadcasted_iota(jnp.int32, (NB, NB), 0)
    for r in range(OBS // NB):
        off = off_ref[r : r + 1, :]
        sigma = sigma_ref[r : r + 1, :]
        w = 1.0 / (sigma * sigma)
        s = data_ref[r : r + 1, :] * w
        mask = lax.shift_right_logical(off, 7) == hi_iota
        cols = slice(r * NB, (r + 1) * NB)
        v = [x.astype(F32) for x in split3(w) + split3(s)]
        blocks = [jnp.where(mask, jnp.where(lower, v[2 * i], v[2 * i + 1]), 0.0) for i in range(3)]
        lhs[:, cols] = jnp.concatenate(blocks + [jnp.zeros((8, NB), F32)], axis=0).astype(BF)
        oh[:, cols] = jnp.where((off & 127) == lo_iota, 1.0, 0.0).astype(BF)
    t = lax.dot_general(lhs[...], oh[...], NTDOT, preferred_element_type=F32)
    w = t[0:4] + t[4:8] + t[8:12]
    s = t[12:16] + t[16:20] + t[20:24]
    out_ref[...] = jnp.zeros_like(out_ref)
    for h in range(PART_HI):
        out_ref[0:1, h * NB : (h + 1) * NB] = w[h : h + 1]
        out_ref[1:2, h * NB : (h + 1) * NB] = s[h : h + 1]


def obs_sums(scal, off, data, sigma):
    shape = (OBS // NB, NB)
    return pl.pallas_call(
        obs_kernel,
        out_shape=jax.ShapeDtypeStruct((8, PART), F32),
        in_specs=[SMEM, VMEM, VMEM, VMEM],
        out_specs=VMEM,
        scratch_shapes=[pltpu.VMEM((32, OBS), BF), pltpu.VMEM((NB, OBS), BF)],
        compiler_params=params(24),
        cost_estimate=pl.CostEstimate(flops=2 * 32 * NB * OBS, bytes_accessed=200000, transcendentals=0),
        name="obs_sums",
    )(scal, off.reshape(shape), data.reshape(shape), sigma.reshape(shape))


def blocks_of(core):
    return [(4 * core + i, d) for d in range(4) for i in range(4)] + [(2 * core + i, 4) for i in range(2)]


def gram_kernel(scal, ws_ref, xa, xb, out_ref, b):
    core = scal[2]
    total = jnp.zeros((1, PART), F32)
    for i in range(NK):
        total = total + jnp.sum(xa[i].astype(F32), axis=0, keepdims=True) + jnp.sum(xb[i].astype(F32), axis=0, keepdims=True)
    mean = total * (1.0 / N)
    w = ws_ref[0:1, :]
    root = jnp.sqrt(w)
    for i in range(NK):
        b[at(2 * i + core, 64), :] = ((xa[i].astype(F32) - mean) * root).astype(BF)
        b[at(2 * i + 1 - core, 64), :] = ((xb[i].astype(F32) - mean) * root).astype(BF)
    d = jnp.where(w > 0.0, (ws_ref[1:2, :] - mean * w) * lax.rsqrt(jnp.where(w > 0.0, w, 1.0)), 0.0)
    d = jnp.concatenate([x.astype(F32) for x in split3(d)] + [jnp.zeros((13, PART), F32)], axis=0).astype(BF)
    drive = lax.dot_general(d, b[...], NTDOT, preferred_element_type=F32)
    drive = jnp.sum(drive, axis=0, keepdims=True)
    drive = jnp.concatenate([drive[:, i * NB : (i + 1) * NB] for i in range(NK)], axis=0)
    for t in range(16):
        out_ref[t, GROWS:, :] = drive
    for n, (i, d) in enumerate(blocks_of(0)):
        i = i + core * (4 if d < 4 else 2)
        g = lax.dot_general(b[at(i, NB), :], b[at((i + d) % NK, NB), :], NTDOT, preferred_element_type=F32)
        row = 0
        while row < NB:
            t, r = divmod(n * NB + row, GROWS)
            size = min(NB - row, GROWS - r)
            out_ref[t, r : r + size, :] = g[row : row + size]
            row += size


def gram_part(scal, ws, xa, xb):
    return pl.pallas_call(
        gram_kernel,
        out_shape=jax.ShapeDtypeStruct((16, GROWS + 8, NB), F32),
        in_specs=[SMEM] + [VMEM] * 3,
        out_specs=VMEM,
        scratch_shapes=[pltpu.VMEM((N, PART), BF)],
        compiler_params=params(32),
        cost_estimate=pl.CostEstimate(flops=2 * NB * NB * 18 * PART, bytes_accessed=3 * 2**20, transcendentals=0),
        name="gram_part",
    )(scal, ws, xa, xb)


def diag_inverse(dz, vout):
    for j in range(NB // SB):
        r0 = j * SB
        rs = [jnp.broadcast_to(dz[r0 + p : r0 + p + 1, 0:NB], (SB, NB)) for p in range(SB)]
        rw = [jnp.broadcast_to(dz[r0 + p : r0 + p + 1, NB : 2 * NB], (SB, NB)) for p in range(SB)]
        e = [[jnp.broadcast_to(rs[q][:, r0 + p : r0 + p + 1], (SB, NB)) for p in range(q + 1)] for q in range(SB)]
        groups = range(j + 1, NB // SB)
        c = {}
        for g in groups:
            blk = dz[g * SB : (g + 1) * SB, 0:NB]
            c[g] = [jnp.broadcast_to(blk[:, r0 + p : r0 + p + 1], (SB, NB)) for p in range(SB)]
        for p in range(SB):
            r = lax.rsqrt(e[p][p])
            rs[p] = rs[p] * r
            rw[p] = rw[p] * r
            f = {q: e[q][p] * r for q in range(p + 1, SB)}
            for q in range(p + 1, SB):
                for s in range(p + 1, q + 1):
                    e[q][s] = e[q][s] - f[q] * f[s]
            for q in range(p + 1, SB):
                rs[q] = rs[q] - f[q] * rs[p]
                rw[q] = rw[q] - f[q] * rw[p]
            for g in groups:
                c[g][p] = c[g][p] * r
                for q in range(p + 1, SB):
                    c[g][q] = c[g][q] - f[q] * c[g][p]
        for p in range(SB):
            vout[r0 + p : r0 + p + 1, :] = rw[p][0:1, :]
        for g in groups:
            ds = dz[g * SB : (g + 1) * SB, 0:NB]
            dw = dz[g * SB : (g + 1) * SB, NB : 2 * NB]
            for p in range(SB):
                ds = ds - c[g][p] * rs[p]
                dw = dw - c[g][p] * rw[p]
            dz[g * SB : (g + 1) * SB, 0:NB] = ds
            dz[g * SB : (g + 1) * SB, NB : 2 * NB] = dw


def inverse_factor(z, dz, vb, lhs, rhs):
    rows = lax.broadcasted_iota(jnp.int32, (NB, NB), 0)
    eye = jnp.where(rows == lax.broadcasted_iota(jnp.int32, (NB, NB), 1), 1.0, 0.0)
    zero = jnp.zeros((NB, NB), F32)

    def step(k, carry):
        ks = at(k, NB)
        dz[:, 0:NB] = z[ks, ks]
        dz[:, NB : 2 * NB] = eye
        diag_inverse(dz, vb)
        v = vb[...]
        vh, vm, vl = split3(v)
        zh, zm, zl = split3(z[ks, :])
        a = jnp.concatenate([vh, vh, vm, vh, vl, vm], axis=1)
        b = jnp.concatenate([zh, zm, zh, zl, zh, zm], axis=0)
        z[ks, :] = jnp.dot(a, b, preferred_element_type=F32)
        z[ks, ks] = v
        rh, rm, rl = split3(z[ks, :])
        for i, x in enumerate([rh, rm, rh, rl, rh, rm]):
            rhs[i * NB : (i + 1) * NB, :] = x
        for i, x in enumerate([rh, rh, rm, rh, rl, rm]):
            lhs[i * NB : (i + 1) * NB, :] = x

        def trail(i, carry):
            si = at(i, NB)
            z[si, ks] = zero
            z[si, :] = z[si, :] - lax.dot_general(lhs[:, si], rhs[...], TNDOT, preferred_element_type=F32)
            z[ks, si] = zero
            return carry

        return lax.fori_loop(k + 1, NK, trail, carry)

    lax.fori_loop(0, NK, step, 0)


def transform_kernel(scal, ga, gb, drive_ref, t_ref, corr_ref, z, dz, vb, lhs, rhs):
    core = scal[2]
    me = scal[0] * 4 + scal[1]
    rows = lax.broadcasted_iota(jnp.int32, (NB, NB), 0)
    ridge = jnp.where(rows == lax.broadcasted_iota(jnp.int32, (NB, NB), 1), N - 1.0, 0.0)
    zero_core = (rows * 0 + core) == 0
    for c in range(2):
        for n, (i, d) in enumerate(blocks_of(c)):
            j = i + d
            a = ga[n * NB : (n + 1) * NB, :]
            b = gb[n * NB : (n + 1) * NB, :]
            blk = jnp.where(zero_core, a, b) if c == 0 else jnp.where(zero_core, b, a)
            if d == 0:
                z[i * NB : (i + 1) * NB, i * NB : (i + 1) * NB] = blk + ridge
            elif j < NK:
                z[i * NB : (i + 1) * NB, j * NB : (j + 1) * NB] = blk
            else:
                z[(j - NK) * NB : (j - NK + 1) * NB, i * NB : (i + 1) * NB] = blk.T
    inverse_factor(z, dz, vb, lhs, rhs)
    drive = jnp.concatenate([drive_ref[i : i + 1, :] for i in range(NK)], axis=1)

    def weigh(i, acc):
        x = z[at(i, 64), :]
        x = x * jnp.sum(x * drive, axis=1, keepdims=True)
        for q in range(8):
            acc = acc + x[q * 8 : (q + 1) * 8]
        return acc

    weights = jnp.sum(lax.fori_loop(0, N // 64, weigh, jnp.zeros((8, N), F32)), axis=0, keepdims=True)
    own = jnp.concatenate([z[at(2 * me + core, 64), :], z[at(2 * me + 1 - core, 64), :]], axis=0)
    t = (own * math.sqrt(N - 1) + weights).astype(BF)
    t_ref[0:NB, :] = t
    t_ref[NB:, :] = jnp.full((16, N), 1.0 / N, BF)
    corr_ref[...] = jnp.broadcast_to(1.0 - jnp.sum(t.astype(F32), axis=1, keepdims=True), corr_ref.shape)


def transform(scal, ga, gb, drive):
    return pl.pallas_call(
        transform_kernel,
        out_shape=(jax.ShapeDtypeStruct((NB + 16, N), BF), jax.ShapeDtypeStruct((NB, NB), F32)),
        in_specs=[SMEM, VMEM, VMEM, VMEM],
        out_specs=(VMEM, VMEM),
        scratch_shapes=[
            pltpu.VMEM((N, N), F32),
            pltpu.VMEM((NB, 2 * NB), F32),
            pltpu.VMEM((NB, NB), F32),
            pltpu.VMEM((6 * NB, N), BF),
            pltpu.VMEM((6 * NB, N), BF),
        ],
        compiler_params=params(40),
        cost_estimate=pl.CostEstimate(flops=10**10, bytes_accessed=4 * 2**20, transcendentals=0),
        name="transform",
    )(scal, ga, gb, drive)


def update_kernel(t_ref, corr_ref, x_ref, keep, send):
    acc = jnp.dot(t_ref[...], x_ref[...], preferred_element_type=F32)
    acc = acc[:NB] + corr_ref[:, 0:1] * acc[NB : NB + 1]
    keep[...] = acc[:64].astype(BF)
    send[...] = acc[64:].astype(BF)


def update(t, corr, x):
    part = jax.ShapeDtypeStruct((64, HALF), BF)
    width = 512
    out = pl.BlockSpec((64, width), lambda i: (0, i))
    return pl.pallas_call(
        update_kernel,
        grid=(HALF // width,),
        out_shape=(part, part),
        in_specs=[
            pl.BlockSpec((NB + 16, N), lambda i: (0, 0)),
            pl.BlockSpec((NB, NB), lambda i: (0, 0)),
            pl.BlockSpec((N, width), lambda i: (0, i)),
        ],
        out_specs=(out, out),
        compiler_params=params(32),
        cost_estimate=pl.CostEstimate(flops=2 * NB * N * HALF, bytes_accessed=5 * 2**20, transcendentals=0),
        name="update",
    )(t, corr, x)


def swap(x):
    return lax.ppermute(x, "core", [(0, 1), (1, 0)])


CHIPS = ("yh", "x")
PLANE = ("yh", "x", "yl")


def gather(x, axes, size):
    return lax.all_to_all(jnp.broadcast_to(x[None], (size, *x.shape)), axes, 0, 0, tiled=True)


def per_device(background_samples, sensor_cell_offsets, sensor_data, sensor_sigma_list):
    core = lax.axis_index("core")
    scal = jnp.stack([lax.axis_index("yh"), lax.axis_index("x"), core]).astype(jnp.int32)
    xa = lax.all_to_all(background_samples.reshape(64, NK, PART), CHIPS, 1, 0)
    xb = swap(xa)
    first = core == 0
    low, high = background_samples[:, :HALF], background_samples[:, HALF:]
    mine = jnp.where(first, low, high)
    got = swap(jnp.where(first, high, low))
    block = jnp.where(first, jnp.concatenate([mine, got]), jnp.concatenate([got, mine]))
    samples = lax.all_gather(block, CHIPS, axis=0, tiled=True)
    ws = obs_sums(scal, sensor_cell_offsets, sensor_data, sensor_sigma_list)
    part = gram_part(scal, ws, xa, xb)
    part = jnp.sum(lax.all_to_all(part, PLANE, 0, 0, tiled=True), axis=0)
    part = jnp.pad(part, ((0, 40), (0, 0))).reshape(8, 24, NB)
    part = jnp.sum(lax.all_to_all(part, ("z",), 0, 0, tiled=True), axis=0)
    part = gather(part, ("z",), 8).reshape(192, NB)
    ga = gather(part[:GROWS], PLANE, 16).reshape(16 * GROWS, NB)
    gb = swap(ga)
    t, corr = transform(scal, ga, gb, part[GROWS : GROWS + 8])
    keep, send = update(t, corr, samples)
    got = swap(send)
    return jnp.where(first, jnp.concatenate([keep, got], axis=1), jnp.concatenate([got, keep], axis=1))


def solution(mesh):
    names = ("yh", "x", "core", "z", "yl")
    split = Mesh(mesh.devices.reshape(2, 4, 2, 8, 2), names)
    mem, sp = names[:3], names[3:]
    return jax.shard_map(
        per_device,
        mesh=split,
        in_specs=(P(mem, sp), P(sp), P(sp), P(sp)),
        out_specs=P(mem, sp),
        check_vma=False,
    )
```

```python
import math

import jax
import jax.numpy as jnp
from jax import lax
from jax.experimental import pallas as pl
from jax.experimental.pallas import tpu as pltpu
from jax.sharding import Mesh, PartitionSpec as P

F32 = jnp.float32
BF = jnp.bfloat16
N = 1024
CELLS = 4096
OBS = 8192
NB = 128
SB = 8
NK = N // NB
PART = CELLS // NK
PART_HI = PART // NB
GROWS = 144
VMEM = pl.BlockSpec(memory_space=pltpu.VMEM)
SMEM = pl.BlockSpec(memory_space=pltpu.SMEM)
NTDOT = (((1,), (1,)), ((), ()))
TNDOT = (((0,), (0,)), ((), ()))


def params(mib):
    return pltpu.CompilerParams(vmem_limit_bytes=mib * 2**20)


def split3(x):
    h = x.astype(BF)
    r = x - h.astype(F32)
    m = r.astype(BF)
    return h, m, (r - m.astype(F32)).astype(BF)


def at(i, size):
    return pl.ds(pl.multiple_of(i * size, size), size)


def obs_kernel(scal, off_ref, data_ref, sigma_ref, out_ref, lhs, oh):
    first = (scal[0] * 4 + scal[1]) * PART_HI
    row = lax.broadcasted_iota(jnp.int32, (8, NB), 0)
    hi_iota = (row & 3) + first
    lower = row < 4
    lo_iota = lax.broadcasted_iota(jnp.int32, (NB, NB), 0)
    for r in range(OBS // NB):
        off = off_ref[r : r + 1, :]
        sigma = sigma_ref[r : r + 1, :]
        w = 1.0 / (sigma * sigma)
        s = data_ref[r : r + 1, :] * w
        mask = lax.shift_right_logical(off, 7) == hi_iota
        cols = slice(r * NB, (r + 1) * NB)
        v = [x.astype(F32) for x in split3(w) + split3(s)]
        blocks = [jnp.where(mask, jnp.where(lower, v[2 * i], v[2 * i + 1]), 0.0) for i in range(3)]
        lhs[:, cols] = jnp.concatenate(blocks + [jnp.zeros((8, NB), F32)], axis=0).astype(BF)
        oh[:, cols] = jnp.where((off & 127) == lo_iota, 1.0, 0.0).astype(BF)
    t = lax.dot_general(lhs[...], oh[...], NTDOT, preferred_element_type=F32)
    w = t[0:4] + t[4:8] + t[8:12]
    s = t[12:16] + t[16:20] + t[20:24]
    out_ref[...] = jnp.zeros_like(out_ref)
    for h in range(PART_HI):
        out_ref[0:1, h * NB : (h + 1) * NB] = w[h : h + 1]
        out_ref[1:2, h * NB : (h + 1) * NB] = s[h : h + 1]


def obs_sums(scal, off, data, sigma):
    shape = (OBS // NB, NB)
    return pl.pallas_call(
        obs_kernel,
        out_shape=jax.ShapeDtypeStruct((8, PART), F32),
        in_specs=[SMEM, VMEM, VMEM, VMEM],
        out_specs=VMEM,
        scratch_shapes=[pltpu.VMEM((32, OBS), BF), pltpu.VMEM((NB, OBS), BF)],
        compiler_params=params(24),
        cost_estimate=pl.CostEstimate(flops=2 * 32 * NB * OBS, bytes_accessed=200000, transcendentals=0),
        name="obs_sums",
    )(scal, off.reshape(shape), data.reshape(shape), sigma.reshape(shape))


def blocks_of(core):
    return [(4 * core + i, d) for d in range(4) for i in range(4)] + [(2 * core + i, 4) for i in range(2)]


def gram_kernel(scal, ws_ref, xa, xb, out_ref, mean_ref, b):
    core = scal[2]
    total = jnp.zeros((1, PART), F32)
    for i in range(NK):
        total = total + jnp.sum(xa[i].astype(F32), axis=0, keepdims=True) + jnp.sum(xb[i].astype(F32), axis=0, keepdims=True)
    mean = total * (1.0 / N)
    mean_ref[...] = jnp.broadcast_to(mean, (8, PART))
    w = ws_ref[0:1, :]
    root = jnp.sqrt(w)
    for i in range(NK):
        b[at(2 * i + core, 64), :] = ((xa[i].astype(F32) - mean) * root).astype(BF)
        b[at(2 * i + 1 - core, 64), :] = ((xb[i].astype(F32) - mean) * root).astype(BF)
    d = jnp.where(w > 0.0, (ws_ref[1:2, :] - mean * w) * lax.rsqrt(jnp.where(w > 0.0, w, 1.0)), 0.0)
    d = jnp.concatenate([x.astype(F32) for x in split3(d)] + [jnp.zeros((13, PART), F32)], axis=0).astype(BF)
    drive = lax.dot_general(d, b[...], NTDOT, preferred_element_type=F32)
    drive = jnp.sum(drive, axis=0, keepdims=True)
    drive = jnp.concatenate([drive[:, i * NB : (i + 1) * NB] for i in range(NK)], axis=0)
    for t in range(16):
        out_ref[t, GROWS:, :] = drive
    for n, (i, d) in enumerate(blocks_of(0)):
        i = i + core * (4 if d < 4 else 2)
        g = lax.dot_general(b[at(i, NB), :], b[at((i + d) % NK, NB), :], NTDOT, preferred_element_type=F32)
        row = 0
        while row < NB:
            t, r = divmod(n * NB + row, GROWS)
            size = min(NB - row, GROWS - r)
            out_ref[t, r : r + size, :] = g[row : row + size]
            row += size


def gram_part(scal, ws, xa, xb):
    return pl.pallas_call(
        gram_kernel,
        out_shape=(jax.ShapeDtypeStruct((16, GROWS + 8, NB), F32), jax.ShapeDtypeStruct((8, PART), F32)),
        in_specs=[SMEM] + [VMEM] * 3,
        out_specs=(VMEM, VMEM),
        scratch_shapes=[pltpu.VMEM((N, PART), BF)],
        compiler_params=params(32),
        cost_estimate=pl.CostEstimate(flops=2 * NB * NB * 18 * PART, bytes_accessed=3 * 2**20, transcendentals=0),
        name="gram_part",
    )(scal, ws, xa, xb)


def diag_inverse(dz, vout):
    for j in range(NB // SB):
        r0 = j * SB
        rs = [jnp.broadcast_to(dz[r0 + p : r0 + p + 1, 0:NB], (SB, NB)) for p in range(SB)]
        rw = [jnp.broadcast_to(dz[r0 + p : r0 + p + 1, NB : 2 * NB], (SB, NB)) for p in range(SB)]
        e = [[jnp.broadcast_to(rs[q][:, r0 + p : r0 + p + 1], (SB, NB)) for p in range(q + 1)] for q in range(SB)]
        groups = range(j + 1, NB // SB)
        c = {}
        for g in groups:
            blk = dz[g * SB : (g + 1) * SB, 0:NB]
            c[g] = [jnp.broadcast_to(blk[:, r0 + p : r0 + p + 1], (SB, NB)) for p in range(SB)]
        for p in range(SB):
            r = lax.rsqrt(e[p][p])
            rs[p] = rs[p] * r
            rw[p] = rw[p] * r
            f = {q: e[q][p] * r for q in range(p + 1, SB)}
            for q in range(p + 1, SB):
                for s in range(p + 1, q + 1):
                    e[q][s] = e[q][s] - f[q] * f[s]
            for q in range(p + 1, SB):
                rs[q] = rs[q] - f[q] * rs[p]
                rw[q] = rw[q] - f[q] * rw[p]
            for g in groups:
                c[g][p] = c[g][p] * r
                for q in range(p + 1, SB):
                    c[g][q] = c[g][q] - f[q] * c[g][p]
        for p in range(SB):
            vout[r0 + p : r0 + p + 1, :] = rw[p][0:1, :]
        for g in groups:
            ds = dz[g * SB : (g + 1) * SB, 0:NB]
            dw = dz[g * SB : (g + 1) * SB, NB : 2 * NB]
            for p in range(SB):
                ds = ds - c[g][p] * rs[p]
                dw = dw - c[g][p] * rw[p]
            dz[g * SB : (g + 1) * SB, 0:NB] = ds
            dz[g * SB : (g + 1) * SB, NB : 2 * NB] = dw


def inverse_factor(z, dz, vb, lhs, rhs):
    rows = lax.broadcasted_iota(jnp.int32, (NB, NB), 0)
    eye = jnp.where(rows == lax.broadcasted_iota(jnp.int32, (NB, NB), 1), 1.0, 0.0)
    zero = jnp.zeros((NB, NB), F32)

    def step(k, carry):
        ks = at(k, NB)
        dz[:, 0:NB] = z[ks, ks]
        dz[:, NB : 2 * NB] = eye
        diag_inverse(dz, vb)
        v = vb[...]
        vh, vm, vl = split3(v)
        zh, zm, zl = split3(z[ks, :])
        a = jnp.concatenate([vh, vh, vm, vh, vl, vm], axis=1)
        b = jnp.concatenate([zh, zm, zh, zl, zh, zm], axis=0)
        z[ks, :] = jnp.dot(a, b, preferred_element_type=F32)
        z[ks, ks] = v
        rh, rm, rl = split3(z[ks, :])
        for i, x in enumerate([rh, rm, rh, rl, rh, rm]):
            rhs[i * NB : (i + 1) * NB, :] = x
        for i, x in enumerate([rh, rh, rm, rh, rl, rm]):
            lhs[i * NB : (i + 1) * NB, :] = x

        def trail(i, carry):
            si = at(i, NB)
            z[si, ks] = zero
            z[si, :] = z[si, :] - lax.dot_general(lhs[:, si], rhs[...], TNDOT, preferred_element_type=F32)
            z[ks, si] = zero
            return carry

        return lax.fori_loop(k + 1, NK, trail, carry)

    lax.fori_loop(0, NK, step, 0)


def transform_kernel(scal, ga, gb, drive_ref, xa, xb, mean_ref, out_ref, z, dz, vb, lhs, rhs, t, x):
    core = scal[2]
    rows = lax.broadcasted_iota(jnp.int32, (NB, NB), 0)
    ridge = jnp.where(rows == lax.broadcasted_iota(jnp.int32, (NB, NB), 1), N - 1.0, 0.0)
    zero_core = (rows * 0 + core) == 0
    for c in range(2):
        for n, (i, d) in enumerate(blocks_of(c)):
            j = i + d
            a = ga[n * NB : (n + 1) * NB, :]
            b = gb[n * NB : (n + 1) * NB, :]
            blk = jnp.where(zero_core, a, b) if c == 0 else jnp.where(zero_core, b, a)
            if d == 0:
                z[i * NB : (i + 1) * NB, i * NB : (i + 1) * NB] = blk + ridge
            elif j < NK:
                z[i * NB : (i + 1) * NB, j * NB : (j + 1) * NB] = blk
            else:
                z[(j - NK) * NB : (j - NK + 1) * NB, i * NB : (i + 1) * NB] = blk.T
    inverse_factor(z, dz, vb, lhs, rhs)
    drive = jnp.concatenate([drive_ref[i : i + 1, :] for i in range(NK)], axis=1)

    def weigh(i, acc):
        x = z[at(i, 64), :]
        x = x * jnp.sum(x * drive, axis=1, keepdims=True)
        for q in range(8):
            acc = acc + x[q * 8 : (q + 1) * 8]
        return acc

    weights = jnp.sum(lax.fori_loop(0, N // 64, weigh, jnp.zeros((8, N), F32)), axis=0, keepdims=True)
    corr = []
    for i in range(NK):
        own = (z[at(2 * i + core, 64), :] * math.sqrt(N - 1) + weights).astype(BF)
        t[i * 64 : (i + 1) * 64, :] = own
        corr.append(1.0 - jnp.sum(own.astype(F32), axis=1, keepdims=True))
        x[at(2 * i + core, 64), :] = xa[i]
        x[at(2 * i + 1 - core, 64), :] = xb[i]
    for i in range(0, NK, 2):
        y = jnp.dot(t[i * 64 : (i + 2) * 64, :], x[...], preferred_element_type=F32)
        for j in range(2):
            out_ref[i + j] = (y[64 * j : 64 * j + 64] + corr[i + j] * mean_ref[0:1, :]).astype(BF)


def transform(scal, ga, gb, drive, xa, xb, mean):
    return pl.pallas_call(
        transform_kernel,
        out_shape=jax.ShapeDtypeStruct((NK, 64, PART), BF),
        in_specs=[SMEM] + [VMEM] * 6,
        out_specs=VMEM,
        scratch_shapes=[
            pltpu.VMEM((N, N), F32),
            pltpu.VMEM((NB, 2 * NB), F32),
            pltpu.VMEM((NB, NB), F32),
            pltpu.VMEM((6 * NB, N), BF),
            pltpu.VMEM((6 * NB, N), BF),
            pltpu.VMEM((N // 2, N), BF),
            pltpu.VMEM((N, PART), BF),
        ],
        compiler_params=params(40),
        cost_estimate=pl.CostEstimate(flops=10**10, bytes_accessed=4 * 2**20, transcendentals=0),
        name="transform",
    )(scal, ga, gb, drive, xa, xb, mean)


def swap(x):
    return lax.ppermute(x, "core", [(0, 1), (1, 0)])


CHIPS = ("yh", "x")
PLANE = ("yh", "x", "yl")


def gather(x, axes, size):
    return lax.all_to_all(jnp.broadcast_to(x[None], (size, *x.shape)), axes, 0, 0, tiled=True)


def per_device(background_samples, sensor_cell_offsets, sensor_data, sensor_sigma_list):
    core = lax.axis_index("core")
    scal = jnp.stack([lax.axis_index("yh"), lax.axis_index("x"), core]).astype(jnp.int32)
    xa = lax.all_to_all(background_samples.reshape(64, NK, PART), CHIPS, 1, 0)
    xb = swap(xa)
    ws = obs_sums(scal, sensor_cell_offsets, sensor_data, sensor_sigma_list)
    part, mean = gram_part(scal, ws, xa, xb)
    part = jnp.sum(lax.all_to_all(part, PLANE, 0, 0, tiled=True), axis=0)
    part = jnp.pad(part, ((0, 40), (0, 0))).reshape(8, 24, NB)
    part = jnp.sum(lax.all_to_all(part, ("z",), 0, 0, tiled=True), axis=0)
    part = gather(part, ("z",), 8).reshape(192, NB)
    ga = gather(part[:GROWS], PLANE, 16).reshape(16 * GROWS, NB)
    gb = swap(ga)
    out = transform(scal, ga, gb, part[GROWS : GROWS + 8], xa, xb, mean)
    return lax.all_to_all(out, CHIPS, 0, 1).reshape(64, CELLS)


def solution(mesh):
    names = ("yh", "x", "core", "z", "yl")
    split = Mesh(mesh.devices.reshape(2, 4, 2, 8, 2), names)
    mem, sp = names[:3], names[3:]
    return jax.shard_map(
        per_device,
        mesh=split,
        in_specs=(P(mem, sp), P(sp), P(sp), P(sp)),
        out_specs=P(mem, sp),
        check_vma=False,
    )
```

```python
import math

import jax
import jax.numpy as jnp
from jax import lax
from jax.experimental import pallas as pl
from jax.experimental.pallas import tpu as pltpu
from jax.sharding import Mesh, PartitionSpec as P

F32 = jnp.float32
BF = jnp.bfloat16
N = 1024
CELLS = 4096
OBS = 8192
NB = 128
SB = 8
NK = N // NB
PART = CELLS // NK
PART_HI = PART // NB
GROWS = 144
VMEM = pl.BlockSpec(memory_space=pltpu.VMEM)
SMEM = pl.BlockSpec(memory_space=pltpu.SMEM)
NTDOT = (((1,), (1,)), ((), ()))


def params(mib):
    return pltpu.CompilerParams(vmem_limit_bytes=mib * 2**20)


def split3(x):
    h = x.astype(BF)
    r = x - h.astype(F32)
    m = r.astype(BF)
    return h, m, (r - m.astype(F32)).astype(BF)


def at(i, size):
    return pl.ds(pl.multiple_of(i * size, size), size)


def obs_kernel(scal, off_ref, data_ref, sigma_ref, out_ref, lhs, oh):
    first = (scal[0] * 4 + scal[1]) * PART_HI
    row = lax.broadcasted_iota(jnp.int32, (8, NB), 0)
    hi_iota = (row & 3) + first
    lower = row < 4
    lo_iota = lax.broadcasted_iota(jnp.int32, (NB, NB), 0)
    for r in range(OBS // NB):
        off = off_ref[r : r + 1, :]
        sigma = sigma_ref[r : r + 1, :]
        w = 1.0 / (sigma * sigma)
        s = data_ref[r : r + 1, :] * w
        mask = lax.shift_right_logical(off, 7) == hi_iota
        cols = slice(r * NB, (r + 1) * NB)
        v = [x.astype(F32) for x in split3(w) + split3(s)]
        blocks = [jnp.where(mask, jnp.where(lower, v[2 * i], v[2 * i + 1]), 0.0) for i in range(3)]
        lhs[:, cols] = jnp.concatenate(blocks + [jnp.zeros((8, NB), F32)], axis=0).astype(BF)
        oh[:, cols] = jnp.where((off & 127) == lo_iota, 1.0, 0.0).astype(BF)
    t = lax.dot_general(lhs[...], oh[...], NTDOT, preferred_element_type=F32)
    w = t[0:4] + t[4:8] + t[8:12]
    s = t[12:16] + t[16:20] + t[20:24]
    out_ref[...] = jnp.zeros_like(out_ref)
    for h in range(PART_HI):
        out_ref[0:1, h * NB : (h + 1) * NB] = w[h : h + 1]
        out_ref[1:2, h * NB : (h + 1) * NB] = s[h : h + 1]


def obs_sums(scal, off, data, sigma):
    shape = (OBS // NB, NB)
    return pl.pallas_call(
        obs_kernel,
        out_shape=jax.ShapeDtypeStruct((8, PART), F32),
        in_specs=[SMEM, VMEM, VMEM, VMEM],
        out_specs=VMEM,
        scratch_shapes=[pltpu.VMEM((32, OBS), BF), pltpu.VMEM((NB, OBS), BF)],
        compiler_params=params(24),
        cost_estimate=pl.CostEstimate(flops=2 * 32 * NB * OBS, bytes_accessed=200000, transcendentals=0),
        name="obs_sums",
    )(scal, off.reshape(shape), data.reshape(shape), sigma.reshape(shape))


def blocks_of(core):
    return [(4 * core + i, d) for d in range(4) for i in range(4)] + [(2 * core + i, 4) for i in range(2)]


def gram_kernel(scal, ws_ref, xa, xb, out_ref, mean_ref, b):
    core = scal[2]
    total = jnp.zeros((1, PART), F32)
    for i in range(NK):
        total = total + jnp.sum(xa[i].astype(F32), axis=0, keepdims=True) + jnp.sum(xb[i].astype(F32), axis=0, keepdims=True)
    mean = total * (1.0 / N)
    mean_ref[...] = jnp.broadcast_to(mean, (8, PART))
    w = ws_ref[0:1, :]
    root = jnp.sqrt(w)
    for i in range(NK):
        b[at(2 * i + core, 64), :] = ((xa[i].astype(F32) - mean) * root).astype(BF)
        b[at(2 * i + 1 - core, 64), :] = ((xb[i].astype(F32) - mean) * root).astype(BF)
    d = jnp.where(w > 0.0, (ws_ref[1:2, :] - mean * w) * lax.rsqrt(jnp.where(w > 0.0, w, 1.0)), 0.0)
    d = jnp.concatenate([x.astype(F32) for x in split3(d)] + [jnp.zeros((13, PART), F32)], axis=0).astype(BF)
    drive = lax.dot_general(d, b[...], NTDOT, preferred_element_type=F32)
    drive = jnp.sum(drive, axis=0, keepdims=True)
    drive = jnp.concatenate([drive[:, i * NB : (i + 1) * NB] for i in range(NK)], axis=0)
    for t in range(16):
        out_ref[t, GROWS:, :] = drive
    for n, (i, d) in enumerate(blocks_of(0)):
        i = i + core * (4 if d < 4 else 2)
        g = lax.dot_general(b[at(i, NB), :], b[at((i + d) % NK, NB), :], NTDOT, preferred_element_type=F32)
        row = 0
        while row < NB:
            t, r = divmod(n * NB + row, GROWS)
            size = min(NB - row, GROWS - r)
            out_ref[t, r : r + size, :] = g[row : row + size]
            row += size


def gram_part(scal, ws, xa, xb):
    return pl.pallas_call(
        gram_kernel,
        out_shape=(jax.ShapeDtypeStruct((16, GROWS + 8, NB), F32), jax.ShapeDtypeStruct((8, PART), F32)),
        in_specs=[SMEM] + [VMEM] * 3,
        out_specs=(VMEM, VMEM),
        scratch_shapes=[pltpu.VMEM((N, PART), BF)],
        compiler_params=params(32),
        cost_estimate=pl.CostEstimate(flops=2 * NB * NB * 18 * PART, bytes_accessed=3 * 2**20, transcendentals=0),
        name="gram_part",
    )(scal, ws, xa, xb)


def diag_inverse(dz, vout, thunks):
    steps = NB // SB
    done = 0
    for j in range(steps):
        r0 = j * SB
        rs = [jnp.broadcast_to(dz[r0 + p : r0 + p + 1, 0:NB], (SB, NB)) for p in range(SB)]
        rw = [jnp.broadcast_to(dz[r0 + p : r0 + p + 1, NB : 2 * NB], (SB, NB)) for p in range(SB)]
        e = [[jnp.broadcast_to(rs[q][:, r0 + p : r0 + p + 1], (SB, NB)) for p in range(q + 1)] for q in range(SB)]
        c = {}
        for g in range(j + 1, steps):
            below = dz[g * SB : (g + 1) * SB, 0:NB]
            c[g] = [jnp.broadcast_to(below[:, r0 + p : r0 + p + 1], (SB, NB)) for p in range(SB)]

        def subtract(g, s, w):
            ds = dz[g * SB : (g + 1) * SB, 0:NB]
            dw = dz[g * SB : (g + 1) * SB, NB : 2 * NB]
            for p in range(SB):
                ds = ds - c[g][p] * s[p]
                dw = dw - c[g][p] * w[p]
            dz[g * SB : (g + 1) * SB, 0:NB] = ds
            dz[g * SB : (g + 1) * SB, NB : 2 * NB] = dw

        following = range(j + 1, min(j + 2, steps))
        f, r = [], []
        for p in range(SB):
            r.append(lax.rsqrt(e[p][p]))
            rs[p] = rs[p] * r[p]
            rw[p] = rw[p] * r[p]
            f.append({q: e[q][p] * r[p] for q in range(p + 1, SB)})
            for q in range(p + 1, SB):
                for s in range(p + 1, q + 1):
                    e[q][s] = e[q][s] - f[p][q] * f[p][s]
            for q in range(p + 1, SB):
                rs[q] = rs[q] - f[p][q] * rs[p]
                rw[q] = rw[q] - f[p][q] * rw[p]
            for g in following:
                c[g][p] = c[g][p] * r[p]
                for q in range(p + 1, SB):
                    c[g][q] = c[g][q] - f[p][q] * c[g][p]
        for p in range(SB):
            vout[r0 + p : r0 + p + 1, :] = rw[p][0:1, :]
        for g in following:
            subtract(g, rs, rw)
        if j + 2 < steps:
            for v in (rs, rw):
                for p in range(SB - 1, -1, -1):
                    for q in range(p + 1, SB):
                        v[p] = v[p] - f[p][q] * v[q]
                    v[p] = v[p] * r[p]
            for g in range(j + 2, steps):
                subtract(g, rs, rw)
        while done < len(thunks) * (j + 1) // steps:
            thunks[done]()
            done += 1


def blk(i, n=1):
    return slice(i * NB, (i + n) * NB)


def inverse_factor(z, dz, vb, lhs, rhs):
    rows = lax.broadcasted_iota(jnp.int32, (NB, NB), 0)
    eye = jnp.where(rows == lax.broadcasted_iota(jnp.int32, (NB, NB), 1), 1.0, 0.0)
    pending = []
    for k in range(NK):
        dz[:, 0:NB] = z[blk(k), blk(k)]
        dz[:, NB : 2 * NB] = eye
        diag_inverse(dz, vb, pending)
        pending = []
        v = vb[...]
        side = k % 2
        vh, vm, vl = split3(v)
        a = jnp.concatenate([vh, vh, vm, vh, vl, vm], axis=1)

        def put(j, n, r):
            h, m, l = split3(r)
            for i, x in enumerate([h, m, h, l, h, m]):
                rhs[side, blk(i), blk(j, n)] = x

        def row(j, n):
            h, m, l = split3(z[blk(k), blk(j, n)])
            r = jnp.dot(a, jnp.concatenate([h, m, h, l, h, m], axis=0), preferred_element_type=F32)
            put(j, n, r)
            return r

        z[blk(k), blk(k)] = v
        put(k, 1, v)
        for j in range(0, k, 2):
            n = min(2, k - j)
            z[blk(k), blk(j, n)] = row(j, n)
        for j in range(k + 1, NK, 2):
            n = min(2, NK - j)
            r = row(j, n)
            for q in range(n):
                x = split3(r[:, blk(q)].T)
                for i, t in enumerate([0, 0, 1, 0, 2, 1]):
                    lhs[side, blk(j + q), blk(i)] = x[t]

        def reduce(i, m, j, n, side=side):
            prod = jnp.dot(lhs[side, blk(i, m), :], rhs[side, :, blk(j, n)], preferred_element_type=F32)
            z[blk(i, m), blk(j, n)] = z[blk(i, m), blk(j, n)] - prod

        def later(*args):
            pending.append(lambda: reduce(*args))

        if k + 1 < NK:
            for j in range(0, k + 1, 2):
                reduce(k + 1, 1, j, min(2, k + 1 - j))
            for j in range(k + 1, NK, 2):
                reduce(k + 1, 1, j, min(2, NK - j))
        for j in range(0, k + 1, 2):
            for i in range(k + 2, NK, 3):
                later(i, min(3, NK - i), j, min(2, k + 1 - j), side)
        for j in range(k + 2, NK, 2):
            n = min(2, NK - j)
            for i in range(k + 2, j + 1, 3):
                later(i, min(3, j + 1 - i), j, n, side)
            if n == 2:
                later(j + 1, 1, j + 1, 1, side)


def transform_kernel(scal, ga, gb, drive_ref, xa, xb, mean_ref, out_ref, z, dz, vb, lhs, rhs, t, x):
    core = scal[2]
    rows = lax.broadcasted_iota(jnp.int32, (NB, NB), 0)
    ridge = jnp.where(rows == lax.broadcasted_iota(jnp.int32, (NB, NB), 1), N - 1.0, 0.0)
    zero_core = (rows * 0 + core) == 0
    for i in range(1, NK):
        z[blk(i), 0 : i * NB] = jnp.zeros((NB, i * NB), F32)
    for c in range(2):
        for n, (i, d) in enumerate(blocks_of(c)):
            j = i + d
            a = ga[blk(n), :]
            b = gb[blk(n), :]
            g = jnp.where(zero_core, a, b) if c == 0 else jnp.where(zero_core, b, a)
            if d == 0:
                z[blk(i), blk(i)] = g + ridge
            elif j < NK:
                z[blk(i), blk(j)] = g
            else:
                z[blk(j - NK), blk(i)] = g.T
    inverse_factor(z, dz, vb, lhs, rhs)
    drive = jnp.concatenate([drive_ref[i : i + 1, :] for i in range(NK)], axis=1)
    sums = [jnp.zeros((8, NB), F32) for _ in range(NK)]
    for i in range(NK):
        width = (i + 1) * NB
        for h in range(2):
            y = z[i * NB + 64 * h : i * NB + 64 * h + 64, 0:width]
            y = y * jnp.sum(y * drive[:, 0:width], axis=1, keepdims=True)
            for q in range(8):
                for j in range(i + 1):
                    sums[j] = sums[j] + y[q * 8 : (q + 1) * 8, blk(j)]
    weights = jnp.sum(jnp.concatenate(sums, axis=1), axis=0, keepdims=True)
    corr = []
    for i in range(NK):
        own = z[at(2 * i + core, 64), 0 : (i + 1) * NB] * math.sqrt(N - 1)
        if i + 1 < NK:
            own = jnp.concatenate([own, jnp.zeros((64, N - (i + 1) * NB), F32)], axis=1)
        own = (own + weights).astype(BF)
        t[i * 64 : (i + 1) * 64, :] = own
        corr.append(1.0 - jnp.sum(own.astype(F32), axis=1, keepdims=True))
        x[at(2 * i + core, 64), :] = xa[i]
        x[at(2 * i + 1 - core, 64), :] = xb[i]
    for i in range(0, NK, 2):
        y = jnp.dot(t[i * 64 : (i + 2) * 64, :], x[...], preferred_element_type=F32)
        for j in range(2):
            out_ref[i + j] = (y[64 * j : 64 * j + 64] + corr[i + j] * mean_ref[0:1, :]).astype(BF)


def transform(scal, ga, gb, drive, xa, xb, mean):
    return pl.pallas_call(
        transform_kernel,
        out_shape=jax.ShapeDtypeStruct((NK, 64, PART), BF),
        in_specs=[SMEM] + [VMEM] * 6,
        out_specs=VMEM,
        scratch_shapes=[
            pltpu.VMEM((N, N), F32),
            pltpu.VMEM((NB, 2 * NB), F32),
            pltpu.VMEM((NB, NB), F32),
            pltpu.VMEM((2, N, 6 * NB), BF),
            pltpu.VMEM((2, 6 * NB, N), BF),
            pltpu.VMEM((N // 2, N), BF),
            pltpu.VMEM((N, PART), BF),
        ],
        compiler_params=params(40),
        cost_estimate=pl.CostEstimate(flops=10**10, bytes_accessed=4 * 2**20, transcendentals=0),
        name="transform",
    )(scal, ga, gb, drive, xa, xb, mean)


def swap(x):
    return lax.ppermute(x, "core", [(0, 1), (1, 0)])


CHIPS = ("yh", "x")
PLANE = ("yh", "x", "yl")


def gather(x, axes, size):
    return lax.all_to_all(jnp.broadcast_to(x[None], (size, *x.shape)), axes, 0, 0, tiled=True)


def per_device(background_samples, sensor_cell_offsets, sensor_data, sensor_sigma_list):
    core = lax.axis_index("core")
    scal = jnp.stack([lax.axis_index("yh"), lax.axis_index("x"), core]).astype(jnp.int32)
    xa = lax.all_to_all(background_samples.reshape(64, NK, PART), CHIPS, 1, 0)
    xb = swap(xa)
    ws = obs_sums(scal, sensor_cell_offsets, sensor_data, sensor_sigma_list)
    part, mean = gram_part(scal, ws, xa, xb)
    part = jnp.sum(lax.all_to_all(part, PLANE, 0, 0, tiled=True), axis=0)
    part = jnp.pad(part, ((0, 40), (0, 0))).reshape(8, 24, NB)
    part = jnp.sum(lax.all_to_all(part, ("z",), 0, 0, tiled=True), axis=0)
    part = gather(part, ("z",), 8).reshape(192, NB)
    ga = gather(part[:GROWS], PLANE, 16).reshape(16 * GROWS, NB)
    gb = swap(ga)
    out = transform(scal, ga, gb, part[GROWS : GROWS + 8], xa, xb, mean)
    return lax.all_to_all(out, CHIPS, 0, 1).reshape(64, CELLS)


def solution(mesh):
    names = ("yh", "x", "core", "z", "yl")
    split = Mesh(mesh.devices.reshape(2, 4, 2, 8, 2), names)
    mem, sp = names[:3], names[3:]
    return jax.shard_map(
        per_device,
        mesh=split,
        in_specs=(P(mem, sp), P(sp), P(sp), P(sp)),
        out_specs=P(mem, sp),
        check_vma=False,
    )
```

```python
import math

import jax
import jax.numpy as jnp
from jax import lax
from jax.experimental import pallas as pl
from jax.experimental.pallas import tpu as pltpu
from jax.sharding import Mesh, PartitionSpec as P

F32 = jnp.float32
BF = jnp.bfloat16
N = 1024
CELLS = 4096
OBS = 8192
NB = 128
SB = 8
NK = N // NB
PART = CELLS // NK
PART_HI = PART // NB
GROWS = 144
VMEM = pl.BlockSpec(memory_space=pltpu.VMEM)
SMEM = pl.BlockSpec(memory_space=pltpu.SMEM)
NTDOT = (((1,), (1,)), ((), ()))


def params(mib):
    return pltpu.CompilerParams(vmem_limit_bytes=mib * 2**20)


def split3(x):
    h = x.astype(BF)
    r = x - h.astype(F32)
    m = r.astype(BF)
    return h, m, (r - m.astype(F32)).astype(BF)


def at(i, size):
    return pl.ds(pl.multiple_of(i * size, size), size)


def obs_kernel(scal, off_ref, data_ref, sigma_ref, out_ref, lhs, oh):
    first = (scal[0] * 4 + scal[1]) * PART_HI
    row = lax.broadcasted_iota(jnp.int32, (8, NB), 0)
    hi_iota = (row & 3) + first
    lower = row < 4
    lo_iota = lax.broadcasted_iota(jnp.int32, (NB, NB), 0)
    for r in range(OBS // NB):
        off = off_ref[r : r + 1, :]
        sigma = sigma_ref[r : r + 1, :]
        w = 1.0 / (sigma * sigma)
        s = data_ref[r : r + 1, :] * w
        mask = lax.shift_right_logical(off, 7) == hi_iota
        cols = slice(r * NB, (r + 1) * NB)
        v = [x.astype(F32) for x in split3(w) + split3(s)]
        blocks = [jnp.where(mask, jnp.where(lower, v[2 * i], v[2 * i + 1]), 0.0) for i in range(3)]
        lhs[:, cols] = jnp.concatenate(blocks + [jnp.zeros((8, NB), F32)], axis=0).astype(BF)
        oh[:, cols] = jnp.where((off & 127) == lo_iota, 1.0, 0.0).astype(BF)
    t = lax.dot_general(lhs[...], oh[...], NTDOT, preferred_element_type=F32)
    w = t[0:4] + t[4:8] + t[8:12]
    s = t[12:16] + t[16:20] + t[20:24]
    out_ref[...] = jnp.zeros_like(out_ref)
    for h in range(PART_HI):
        out_ref[0:1, h * NB : (h + 1) * NB] = w[h : h + 1]
        out_ref[1:2, h * NB : (h + 1) * NB] = s[h : h + 1]


def obs_sums(scal, off, data, sigma):
    shape = (OBS // NB, NB)
    return pl.pallas_call(
        obs_kernel,
        out_shape=jax.ShapeDtypeStruct((8, PART), F32),
        in_specs=[SMEM, VMEM, VMEM, VMEM],
        out_specs=VMEM,
        scratch_shapes=[pltpu.VMEM((32, OBS), BF), pltpu.VMEM((NB, OBS), BF)],
        compiler_params=params(24),
        cost_estimate=pl.CostEstimate(flops=2 * 32 * NB * OBS, bytes_accessed=200000, transcendentals=0),
        name="obs_sums",
    )(scal, off.reshape(shape), data.reshape(shape), sigma.reshape(shape))


def blocks_of(core):
    return [(4 * core + i, d) for d in range(4) for i in range(4)] + [(2 * core + i, 4) for i in range(2)]


def gram_kernel(scal, ws_ref, xa, xb, out_ref, mean_ref, b):
    core = scal[2]
    total = jnp.zeros((1, PART), F32)
    for i in range(NK):
        total = total + jnp.sum(xa[i].astype(F32), axis=0, keepdims=True) + jnp.sum(xb[i].astype(F32), axis=0, keepdims=True)
    mean = total * (1.0 / N)
    mean_ref[...] = jnp.broadcast_to(mean, (8, PART))
    w = ws_ref[0:1, :]
    root = jnp.sqrt(w)
    for i in range(NK):
        b[at(2 * i + core, 64), :] = ((xa[i].astype(F32) - mean) * root).astype(BF)
        b[at(2 * i + 1 - core, 64), :] = ((xb[i].astype(F32) - mean) * root).astype(BF)
    d = jnp.where(w > 0.0, (ws_ref[1:2, :] - mean * w) * lax.rsqrt(jnp.where(w > 0.0, w, 1.0)), 0.0)
    d = jnp.concatenate([x.astype(F32) for x in split3(d)] + [jnp.zeros((13, PART), F32)], axis=0).astype(BF)
    drive = lax.dot_general(d, b[...], NTDOT, preferred_element_type=F32)
    drive = jnp.sum(drive, axis=0, keepdims=True)
    drive = jnp.concatenate([drive[:, i * NB : (i + 1) * NB] for i in range(NK)], axis=0)
    for t in range(16):
        out_ref[t, GROWS:, :] = drive
    for n, (i, d) in enumerate(blocks_of(0)):
        i = i + core * (4 if d < 4 else 2)
        g = lax.dot_general(b[at(i, NB), :], b[at((i + d) % NK, NB), :], NTDOT, preferred_element_type=F32)
        row = 0
        while row < NB:
            t, r = divmod(n * NB + row, GROWS)
            size = min(NB - row, GROWS - r)
            out_ref[t, r : r + size, :] = g[row : row + size]
            row += size


def gram_part(scal, ws, xa, xb):
    return pl.pallas_call(
        gram_kernel,
        out_shape=(jax.ShapeDtypeStruct((16, GROWS + 8, NB), F32), jax.ShapeDtypeStruct((8, PART), F32)),
        in_specs=[SMEM] + [VMEM] * 3,
        out_specs=(VMEM, VMEM),
        scratch_shapes=[pltpu.VMEM((N, PART), BF)],
        compiler_params=params(32),
        cost_estimate=pl.CostEstimate(flops=2 * NB * NB * 18 * PART, bytes_accessed=3 * 2**20, transcendentals=0),
        name="gram_part",
    )(scal, ws, xa, xb)


def diag_inverse(dz, vout, eb, thunks):
    steps = NB // SB
    done = 0
    now = dz[0:SB, 0:NB]
    for j in range(steps):
        r0 = j * SB
        rs = [jnp.broadcast_to(dz[r0 + p : r0 + p + 1, 0:NB], (SB, NB)) for p in range(SB)]
        rw = [jnp.broadcast_to(dz[r0 + p : r0 + p + 1, NB : 2 * NB], (SB, NB)) for p in range(SB)]
        for p in range(SB):
            eb[p] = jnp.broadcast_to(now[:, r0 + p : r0 + p + 1], (SB, NB))
        e = [[jnp.broadcast_to(eb[p, q : q + 1, :], (SB, NB)) for p in range(q + 1)] for q in range(SB)]
        c = {}
        for g in range(j + 1, steps):
            below = dz[g * SB : (g + 1) * SB, 0:NB]
            c[g] = [jnp.broadcast_to(below[:, r0 + p : r0 + p + 1], (SB, NB)) for p in range(SB)]

        def subtract(g, s, w):
            ds = dz[g * SB : (g + 1) * SB, 0:NB]
            dw = dz[g * SB : (g + 1) * SB, NB : 2 * NB]
            for p in range(SB):
                ds = ds - c[g][p] * s[p]
                dw = dw - c[g][p] * w[p]
            dz[g * SB : (g + 1) * SB, 0:NB] = ds
            dz[g * SB : (g + 1) * SB, NB : 2 * NB] = dw
            return ds

        following = range(j + 1, min(j + 2, steps))
        f, r = [], []
        for p in range(SB):
            r.append(lax.rsqrt(e[p][p]))
            rs[p] = rs[p] * r[p]
            rw[p] = rw[p] * r[p]
            f.append({q: e[q][p] * r[p] for q in range(p + 1, SB)})
            for q in range(p + 1, SB):
                for s in range(p + 1, q + 1):
                    e[q][s] = e[q][s] - f[p][q] * f[p][s]
            for q in range(p + 1, SB):
                rs[q] = rs[q] - f[p][q] * rs[p]
                rw[q] = rw[q] - f[p][q] * rw[p]
            for g in following:
                c[g][p] = c[g][p] * r[p]
                for q in range(p + 1, SB):
                    c[g][q] = c[g][q] - f[p][q] * c[g][p]
        for p in range(SB):
            vout[r0 + p : r0 + p + 1, :] = rw[p][0:1, :]
        for g in following:
            now = subtract(g, rs, rw)
        if j + 2 < steps:
            for v in (rs, rw):
                for p in range(SB - 1, -1, -1):
                    for q in range(p + 1, SB):
                        v[p] = v[p] - f[p][q] * v[q]
                    v[p] = v[p] * r[p]
            for g in range(j + 2, steps):
                subtract(g, rs, rw)
        while done < len(thunks) * (j + 1) // steps:
            thunks[done]()
            done += 1


def blk(i, n=1):
    return slice(i * NB, (i + n) * NB)


def inverse_factor(z, dz, vb, eb, ab, lhs, rhs):
    rows = lax.broadcasted_iota(jnp.int32, (NB, NB), 0)
    eye = jnp.where(rows == lax.broadcasted_iota(jnp.int32, (NB, NB), 1), 1.0, 0.0)

    def put(side, j, n, r):
        h, m, l = split3(r)
        for i, x in enumerate([h, m, h, l, h, m]):
            rhs[side, blk(i), blk(j, n)] = x

    def own(k):
        v = vb[k % 2]
        z[blk(k), blk(k)] = v
        put(k % 2, k, 1, v)

    def row(k, j, n):
        side = k % 2
        h, m, l = split3(z[blk(k), blk(j, n)])
        r = jnp.dot(ab[side], jnp.concatenate([h, m, h, l, h, m], axis=0), preferred_element_type=F32)
        put(side, j, n, r)
        if j < k:
            z[blk(k), blk(j, n)] = r
            return
        for q in range(n):
            x = split3(r[:, blk(q)].T)
            for i, t in enumerate([0, 0, 1, 0, 2, 1]):
                lhs[side, blk(j + q), blk(i)] = x[t]

    def reduce(side, i, m, j, n):
        prod = jnp.dot(lhs[side, blk(i, m), :], rhs[side, :, blk(j, n)], preferred_element_type=F32)
        z[blk(i, m), blk(j, n)] = z[blk(i, m), blk(j, n)] - prod

    pending = []

    def later(f, *args):
        pending.append(lambda: f(*args))

    for k in range(NK):
        side = k % 2
        dz[:, 0:NB] = z[blk(k), blk(k)]
        dz[:, NB : 2 * NB] = eye
        diag_inverse(dz, vb.at[side], eb.at[side], pending)
        pending.clear()
        h, m, l = split3(vb[side])
        for i, x in enumerate([h, h, m, h, l, m]):
            ab[side, :, blk(i)] = x
        later(own, k)
        if k + 1 < NK:
            row(k, k + 1, 1)
            reduce(side, k + 1, 1, k + 1, 1)
        for j in range(0, k, 2):
            later(row, k, j, min(2, k - j))
        for j in range(k + 2, NK, 2):
            later(row, k, j, min(2, NK - j))
        if k + 1 < NK:
            for j in range(0, k + 1, 2):
                later(reduce, side, k + 1, 1, j, min(2, k + 1 - j))
            for j in range(k + 2, NK, 2):
                later(reduce, side, k + 1, 1, j, min(2, NK - j))
        for j in range(0, k + 1, 2):
            for i in range(k + 2, NK, 3):
                later(reduce, side, i, min(3, NK - i), j, min(2, k + 1 - j))
        for j in range(k + 2, NK, 2):
            n = min(2, NK - j)
            for i in range(k + 2, j + 1, 3):
                later(reduce, side, i, min(3, j + 1 - i), j, n)
            if n == 2:
                later(reduce, side, j + 1, 1, j + 1, 1)
    for f in pending:
        f()


def transform_kernel(scal, ga, gb, drive_ref, xa, xb, mean_ref, out_ref, z, dz, vb, eb, ab, lhs, rhs, t, x):
    core = scal[2]
    rows = lax.broadcasted_iota(jnp.int32, (NB, NB), 0)
    ridge = jnp.where(rows == lax.broadcasted_iota(jnp.int32, (NB, NB), 1), N - 1.0, 0.0)
    zero_core = (rows * 0 + core) == 0
    for i in range(1, NK):
        z[blk(i), 0 : i * NB] = jnp.zeros((NB, i * NB), F32)
    for c in range(2):
        for n, (i, d) in enumerate(blocks_of(c)):
            j = i + d
            a = ga[blk(n), :]
            b = gb[blk(n), :]
            g = jnp.where(zero_core, a, b) if c == 0 else jnp.where(zero_core, b, a)
            if d == 0:
                z[blk(i), blk(i)] = g + ridge
            elif j < NK:
                z[blk(i), blk(j)] = g
            else:
                z[blk(j - NK), blk(i)] = g.T
    inverse_factor(z, dz, vb, eb, ab, lhs, rhs)
    drive = jnp.concatenate([drive_ref[i : i + 1, :] for i in range(NK)], axis=1)
    sums = [jnp.zeros((8, NB), F32) for _ in range(NK)]
    for i in range(NK):
        width = (i + 1) * NB
        for h in range(2):
            y = z[i * NB + 64 * h : i * NB + 64 * h + 64, 0:width]
            y = y * jnp.sum(y * drive[:, 0:width], axis=1, keepdims=True)
            for q in range(8):
                for j in range(i + 1):
                    sums[j] = sums[j] + y[q * 8 : (q + 1) * 8, blk(j)]
    weights = jnp.sum(jnp.concatenate(sums, axis=1), axis=0, keepdims=True)
    corr = []
    for i in range(NK):
        own = z[at(2 * i + core, 64), 0 : (i + 1) * NB] * math.sqrt(N - 1)
        if i + 1 < NK:
            own = jnp.concatenate([own, jnp.zeros((64, N - (i + 1) * NB), F32)], axis=1)
        own = (own + weights).astype(BF)
        t[i * 64 : (i + 1) * 64, :] = own
        corr.append(1.0 - jnp.sum(own.astype(F32), axis=1, keepdims=True))
        x[at(2 * i + core, 64), :] = xa[i]
        x[at(2 * i + 1 - core, 64), :] = xb[i]
    for i in range(0, NK, 2):
        y = jnp.dot(t[i * 64 : (i + 2) * 64, :], x[...], preferred_element_type=F32)
        for j in range(2):
            out_ref[i + j] = (y[64 * j : 64 * j + 64] + corr[i + j] * mean_ref[0:1, :]).astype(BF)


def transform(scal, ga, gb, drive, xa, xb, mean):
    return pl.pallas_call(
        transform_kernel,
        out_shape=jax.ShapeDtypeStruct((NK, 64, PART), BF),
        in_specs=[SMEM] + [VMEM] * 6,
        out_specs=VMEM,
        scratch_shapes=[
            pltpu.VMEM((N, N), F32),
            pltpu.VMEM((NB, 2 * NB), F32),
            pltpu.VMEM((2, NB, NB), F32),
            pltpu.VMEM((2, SB, SB, NB), F32),
            pltpu.VMEM((2, NB, 6 * NB), BF),
            pltpu.VMEM((2, N, 6 * NB), BF),
            pltpu.VMEM((2, 6 * NB, N), BF),
            pltpu.VMEM((N // 2, N), BF),
            pltpu.VMEM((N, PART), BF),
        ],
        compiler_params=params(40),
        cost_estimate=pl.CostEstimate(flops=10**10, bytes_accessed=4 * 2**20, transcendentals=0),
        name="transform",
    )(scal, ga, gb, drive, xa, xb, mean)


def swap(x):
    return lax.ppermute(x, "core", [(0, 1), (1, 0)])


CHIPS = ("yh", "x")
PLANE = ("yh", "x", "yl")


def gather(x, axes, size):
    return lax.all_to_all(jnp.broadcast_to(x[None], (size, *x.shape)), axes, 0, 0, tiled=True)


def per_device(background_samples, sensor_cell_offsets, sensor_data, sensor_sigma_list):
    core = lax.axis_index("core")
    scal = jnp.stack([lax.axis_index("yh"), lax.axis_index("x"), core]).astype(jnp.int32)
    xa = lax.all_to_all(background_samples.reshape(64, NK, PART), CHIPS, 1, 0)
    xb = swap(xa)
    ws = obs_sums(scal, sensor_cell_offsets, sensor_data, sensor_sigma_list)
    part, mean = gram_part(scal, ws, xa, xb)
    part = jnp.sum(lax.all_to_all(part, PLANE, 0, 0, tiled=True), axis=0)
    for step in (1, 2, 4):
        part = part + lax.ppermute(part, "z", [(i, i ^ step) for i in range(8)])
    ga = gather(part[:GROWS], PLANE, 16).reshape(16 * GROWS, NB)
    gb = swap(ga)
    out = transform(scal, ga, gb, part[GROWS : GROWS + 8], xa, xb, mean)
    return lax.all_to_all(out, CHIPS, 0, 1).reshape(64, CELLS)


def solution(mesh):
    names = ("yh", "x", "core", "z", "yl")
    split = Mesh(mesh.devices.reshape(2, 4, 2, 8, 2), names)
    mem, sp = names[:3], names[3:]
    return jax.shard_map(
        per_device,
        mesh=split,
        in_specs=(P(mem, sp), P(sp), P(sp), P(sp)),
        out_specs=P(mem, sp),
        check_vma=False,
    )
```

```python
import math

import jax
import jax.numpy as jnp
from jax import lax
from jax.experimental import pallas as pl
from jax.experimental.pallas import tpu as pltpu
from jax.sharding import Mesh, PartitionSpec as P

F32 = jnp.float32
BF = jnp.bfloat16
N = 1024
CELLS = 4096
OBS = 8192
NB = 128
SB = 8
NK = N // NB
PART = CELLS // NK
PART_HI = PART // NB
GROWS = 144
VMEM = pl.BlockSpec(memory_space=pltpu.VMEM)
SMEM = pl.BlockSpec(memory_space=pltpu.SMEM)
NTDOT = (((1,), (1,)), ((), ()))


def params(mib):
    return pltpu.CompilerParams(vmem_limit_bytes=mib * 2**20)


def split3(x):
    h = x.astype(BF)
    r = x - h.astype(F32)
    m = r.astype(BF)
    return h, m, (r - m.astype(F32)).astype(BF)


def at(i, size):
    return pl.ds(pl.multiple_of(i * size, size), size)


def obs_kernel(scal, off_ref, data_ref, sigma_ref, out_ref, lhs, oh):
    first = (scal[0] * 4 + scal[1]) * PART_HI
    row = lax.broadcasted_iota(jnp.int32, (8, NB), 0)
    hi_iota = (row & 3) + first
    lower = row < 4
    lo_iota = lax.broadcasted_iota(jnp.int32, (NB, NB), 0)
    for r in range(OBS // NB):
        off = off_ref[r : r + 1, :]
        sigma = sigma_ref[r : r + 1, :]
        w = 1.0 / (sigma * sigma)
        s = data_ref[r : r + 1, :] * w
        mask = lax.shift_right_logical(off, 7) == hi_iota
        cols = slice(r * NB, (r + 1) * NB)
        v = [x.astype(F32) for x in split3(w) + split3(s)]
        blocks = [jnp.where(mask, jnp.where(lower, v[2 * i], v[2 * i + 1]), 0.0) for i in range(3)]
        lhs[:, cols] = jnp.concatenate(blocks + [jnp.zeros((8, NB), F32)], axis=0).astype(BF)
        oh[:, cols] = jnp.where((off & 127) == lo_iota, 1.0, 0.0).astype(BF)
    t = lax.dot_general(lhs[...], oh[...], NTDOT, preferred_element_type=F32)
    w = t[0:4] + t[4:8] + t[8:12]
    s = t[12:16] + t[16:20] + t[20:24]
    out_ref[...] = jnp.zeros_like(out_ref)
    for h in range(PART_HI):
        out_ref[0:1, h * NB : (h + 1) * NB] = w[h : h + 1]
        out_ref[1:2, h * NB : (h + 1) * NB] = s[h : h + 1]


def obs_sums(scal, off, data, sigma):
    shape = (OBS // NB, NB)
    return pl.pallas_call(
        obs_kernel,
        out_shape=jax.ShapeDtypeStruct((8, PART), F32),
        in_specs=[SMEM, VMEM, VMEM, VMEM],
        out_specs=VMEM,
        scratch_shapes=[pltpu.VMEM((32, OBS), BF), pltpu.VMEM((NB, OBS), BF)],
        compiler_params=params(24),
        cost_estimate=pl.CostEstimate(flops=2 * 32 * NB * OBS, bytes_accessed=200000, transcendentals=0),
        name="obs_sums",
    )(scal, off.reshape(shape), data.reshape(shape), sigma.reshape(shape))


def blocks_of(core):
    return [(4 * core + i, d) for d in range(4) for i in range(4)] + [(2 * core + i, 4) for i in range(2)]


def gram_kernel(scal, ws_ref, xa, xb, out_ref, mean_ref, b):
    core = scal[2]
    total = jnp.zeros((1, PART), F32)
    for i in range(NK):
        total = total + jnp.sum(xa[i].astype(F32), axis=0, keepdims=True) + jnp.sum(xb[i].astype(F32), axis=0, keepdims=True)
    mean = total * (1.0 / N)
    mean_ref[...] = jnp.broadcast_to(mean, (8, PART))
    w = ws_ref[0:1, :]
    root = jnp.sqrt(w)
    for i in range(NK):
        b[at(2 * i + core, 64), :] = ((xa[i].astype(F32) - mean) * root).astype(BF)
        b[at(2 * i + 1 - core, 64), :] = ((xb[i].astype(F32) - mean) * root).astype(BF)
    d = jnp.where(w > 0.0, (ws_ref[1:2, :] - mean * w) * lax.rsqrt(jnp.where(w > 0.0, w, 1.0)), 0.0)
    d = jnp.concatenate([x.astype(F32) for x in split3(d)] + [jnp.zeros((13, PART), F32)], axis=0).astype(BF)
    drive = lax.dot_general(d, b[...], NTDOT, preferred_element_type=F32)
    drive = jnp.sum(drive, axis=0, keepdims=True)
    drive = jnp.concatenate([drive[:, i * NB : (i + 1) * NB] for i in range(NK)], axis=0)
    for t in range(16):
        out_ref[t, GROWS:, :] = drive
    for n, (i, d) in enumerate(blocks_of(0)):
        i = i + core * (4 if d < 4 else 2)
        g = lax.dot_general(b[at(i, NB), :], b[at((i + d) % NK, NB), :], NTDOT, preferred_element_type=F32)
        row = 0
        while row < NB:
            t, r = divmod(n * NB + row, GROWS)
            size = min(NB - row, GROWS - r)
            out_ref[t, r : r + size, :] = g[row : row + size]
            row += size


def gram_part(scal, ws, xa, xb):
    return pl.pallas_call(
        gram_kernel,
        out_shape=(jax.ShapeDtypeStruct((16, GROWS + 8, NB), F32), jax.ShapeDtypeStruct((8, PART), F32)),
        in_specs=[SMEM] + [VMEM] * 3,
        out_specs=(VMEM, VMEM),
        scratch_shapes=[pltpu.VMEM((N, PART), BF)],
        compiler_params=params(32),
        cost_estimate=pl.CostEstimate(flops=2 * NB * NB * 18 * PART, bytes_accessed=3 * 2**20, transcendentals=0),
        name="gram_part",
    )(scal, ws, xa, xb)


def diag_inverse(dz, vout, eb, thunks):
    steps = NB // SB
    done = 0
    now = dz[0:SB, 0:NB]
    for j in range(steps):
        r0 = j * SB
        rs = [jnp.broadcast_to(dz[r0 + p : r0 + p + 1, 0:NB], (SB, NB)) for p in range(SB)]
        rw = [jnp.broadcast_to(dz[r0 + p : r0 + p + 1, NB : 2 * NB], (SB, NB)) for p in range(SB)]
        for p in range(SB):
            eb[p] = jnp.broadcast_to(now[:, r0 + p : r0 + p + 1], (SB, NB))
        e = [[jnp.broadcast_to(eb[p, q : q + 1, :], (SB, NB)) for p in range(q + 1)] for q in range(SB)]
        c = {}
        for g in range(j + 1, steps):
            below = dz[g * SB : (g + 1) * SB, 0:NB]
            c[g] = [jnp.broadcast_to(below[:, r0 + p : r0 + p + 1], (SB, NB)) for p in range(SB)]

        def subtract(g, s, w):
            ds = dz[g * SB : (g + 1) * SB, 0:NB]
            dw = dz[g * SB : (g + 1) * SB, NB : 2 * NB]
            for p in range(SB):
                ds = ds - c[g][p] * s[p]
                dw = dw - c[g][p] * w[p]
            dz[g * SB : (g + 1) * SB, 0:NB] = ds
            dz[g * SB : (g + 1) * SB, NB : 2 * NB] = dw
            return ds

        following = range(j + 1, min(j + 2, steps))
        f, r = [], []
        for p in range(SB):
            r.append(lax.rsqrt(e[p][p]))
            rs[p] = rs[p] * r[p]
            rw[p] = rw[p] * r[p]
            f.append({q: e[q][p] * r[p] for q in range(p + 1, SB)})
            for q in range(p + 1, SB):
                for s in range(p + 1, q + 1):
                    e[q][s] = e[q][s] - f[p][q] * f[p][s]
            for q in range(p + 1, SB):
                rs[q] = rs[q] - f[p][q] * rs[p]
                rw[q] = rw[q] - f[p][q] * rw[p]
            for g in following:
                c[g][p] = c[g][p] * r[p]
                for q in range(p + 1, SB):
                    c[g][q] = c[g][q] - f[p][q] * c[g][p]
        for p in range(SB):
            vout[r0 + p : r0 + p + 1, :] = rw[p][0:1, :]
        for g in following:
            now = subtract(g, rs, rw)
        if j + 2 < steps:
            for v in (rs, rw):
                for p in range(SB - 1, -1, -1):
                    for q in range(p + 1, SB):
                        v[p] = v[p] - f[p][q] * v[q]
                    v[p] = v[p] * r[p]
            for g in range(j + 2, steps):
                subtract(g, rs, rw)
        while done < len(thunks) * (j + 1) // steps:
            thunks[done]()
            done += 1


def blk(i, n=1):
    return slice(i * NB, (i + n) * NB)


def inverse_factor(z, dz, vb, eb, ab, lhs, rhs):
    rows = lax.broadcasted_iota(jnp.int32, (NB, NB), 0)
    eye = jnp.where(rows == lax.broadcasted_iota(jnp.int32, (NB, NB), 1), 1.0, 0.0)

    def put(side, j, n, r):
        h, m, l = split3(r)
        for i, x in enumerate([h, m, h, l, h, m]):
            rhs[side, blk(i), blk(j, n)] = x

    def own(k):
        v = vb[k % 2]
        z[blk(k), blk(k)] = v
        put(k % 2, k, 1, v)

    def row(k, j, n):
        side = k % 2
        h, m, l = split3(z[blk(k), blk(j, n)])
        r = jnp.dot(ab[side], jnp.concatenate([h, m, h, l, h, m], axis=0), preferred_element_type=F32)
        put(side, j, n, r)
        if j < k:
            z[blk(k), blk(j, n)] = r
            return
        for q in range(n):
            x = split3(r[:, blk(q)].T)
            for i, t in enumerate([0, 0, 1, 0, 2, 1]):
                lhs[side, blk(j + q), blk(i)] = x[t]

    def reduce(side, i, m, j, n):
        prod = jnp.dot(lhs[side, blk(i, m), :], rhs[side, :, blk(j, n)], preferred_element_type=F32)
        z[blk(i, m), blk(j, n)] = z[blk(i, m), blk(j, n)] - prod

    pending = []

    def later(f, *args):
        pending.append(lambda: f(*args))

    for k in range(NK):
        side = k % 2
        dz[:, 0:NB] = z[blk(k), blk(k)]
        dz[:, NB : 2 * NB] = eye
        diag_inverse(dz, vb.at[side], eb.at[side], pending)
        pending.clear()
        h, m, l = split3(vb[side])
        for i, x in enumerate([h, h, m, h, l, m]):
            ab[side, :, blk(i)] = x
        later(own, k)
        if k + 1 < NK:
            row(k, k + 1, 1)
            reduce(side, k + 1, 1, k + 1, 1)
        for j in range(0, k, 2):
            later(row, k, j, min(2, k - j))
        for j in range(k + 2, NK, 2):
            later(row, k, j, min(2, NK - j))
        if k + 1 < NK:
            for j in range(0, k + 1, 2):
                later(reduce, side, k + 1, 1, j, min(2, k + 1 - j))
            for j in range(k + 2, NK, 2):
                later(reduce, side, k + 1, 1, j, min(2, NK - j))
        for j in range(0, k + 1, 2):
            for i in range(k + 2, NK, 3):
                later(reduce, side, i, min(3, NK - i), j, min(2, k + 1 - j))
        for j in range(k + 2, NK, 2):
            n = min(2, NK - j)
            for i in range(k + 2, j + 1, 3):
                later(reduce, side, i, min(3, j + 1 - i), j, n)
            if n == 2:
                later(reduce, side, j + 1, 1, j + 1, 1)
    for f in pending:
        f()


def transform_kernel(scal, ga, gb, drive_ref, xa, xb, mean_ref, out_ref, z, dz, vb, eb, ab, lhs, rhs, t, x):
    core = scal[2]
    rows = lax.broadcasted_iota(jnp.int32, (NB, NB), 0)
    ridge = jnp.where(rows == lax.broadcasted_iota(jnp.int32, (NB, NB), 1), N - 1.0, 0.0)
    zero_core = (rows * 0 + core) == 0
    for i in range(1, NK):
        z[blk(i), 0 : i * NB] = jnp.zeros((NB, i * NB), F32)
    for c in range(2):
        for n, (i, d) in enumerate(blocks_of(c)):
            j = i + d
            a = ga[blk(n), :]
            b = gb[blk(n), :]
            g = jnp.where(zero_core, a, b) if c == 0 else jnp.where(zero_core, b, a)
            if d == 0:
                z[blk(i), blk(i)] = g + ridge
            elif j < NK:
                z[blk(i), blk(j)] = g
            else:
                z[blk(j - NK), blk(i)] = g.T
    inverse_factor(z, dz, vb, eb, ab, lhs, rhs)
    drive = jnp.concatenate([drive_ref[i : i + 1, :] for i in range(NK)], axis=1)
    sums = [jnp.zeros((8, NB), F32) for _ in range(NK)]
    for i in range(NK):
        width = (i + 1) * NB
        for h in range(2):
            y = z[i * NB + 64 * h : i * NB + 64 * h + 64, 0:width]
            y = y * jnp.sum(y * drive[:, 0:width], axis=1, keepdims=True)
            for q in range(8):
                for j in range(i + 1):
                    sums[j] = sums[j] + y[q * 8 : (q + 1) * 8, blk(j)]
    weights = jnp.sum(jnp.concatenate(sums, axis=1), axis=0, keepdims=True)
    corr = []
    for i in range(NK):
        own = z[at(2 * i + core, 64), 0 : (i + 1) * NB] * math.sqrt(N - 1)
        if i + 1 < NK:
            own = jnp.concatenate([own, jnp.zeros((64, N - (i + 1) * NB), F32)], axis=1)
        own = (own + weights).astype(BF)
        t[i * 64 : (i + 1) * 64, :] = own
        corr.append(1.0 - jnp.sum(own.astype(F32), axis=1, keepdims=True))
        x[at(2 * i + core, 64), :] = xa[i]
        x[at(2 * i + 1 - core, 64), :] = xb[i]
    for i in range(0, NK, 2):
        y = jnp.dot(t[i * 64 : (i + 2) * 64, :], x[...], preferred_element_type=F32)
        for j in range(2):
            out_ref[i + j] = (y[64 * j : 64 * j + 64] + corr[i + j] * mean_ref[0:1, :]).astype(BF)


def transform(scal, ga, gb, drive, xa, xb, mean):
    return pl.pallas_call(
        transform_kernel,
        out_shape=jax.ShapeDtypeStruct((NK, 64, PART), BF),
        in_specs=[SMEM] + [VMEM] * 6,
        out_specs=VMEM,
        scratch_shapes=[
            pltpu.VMEM((N, N), F32),
            pltpu.VMEM((NB, 2 * NB), F32),
            pltpu.VMEM((2, NB, NB), F32),
            pltpu.VMEM((2, SB, SB, NB), F32),
            pltpu.VMEM((2, NB, 6 * NB), BF),
            pltpu.VMEM((2, N, 6 * NB), BF),
            pltpu.VMEM((2, 6 * NB, N), BF),
            pltpu.VMEM((N // 2, N), BF),
            pltpu.VMEM((N, PART), BF),
        ],
        compiler_params=params(40),
        cost_estimate=pl.CostEstimate(flops=10**10, bytes_accessed=4 * 2**20, transcendentals=0),
        name="transform",
    )(scal, ga, gb, drive, xa, xb, mean)


def swap(x):
    return lax.ppermute(x, "core", [(0, 1), (1, 0)])


CHIPS = ("yh", "x")
PLANE = ("yh", "x", "yl")


def gather(x, axes, size):
    return lax.all_to_all(jnp.broadcast_to(x[None], (size, *x.shape)), axes, 0, 0, tiled=True)


def per_device(background_samples, sensor_cell_offsets, sensor_data, sensor_sigma_list):
    core = lax.axis_index("core")
    scal = jnp.stack([lax.axis_index("yh"), lax.axis_index("x"), core]).astype(jnp.int32)
    xa = lax.all_to_all(background_samples.reshape(64, NK, PART), CHIPS, 1, 0)
    xb = swap(xa)
    ws = obs_sums(scal, sensor_cell_offsets, sensor_data, sensor_sigma_list)
    part, mean = gram_part(scal, ws, xa, xb)
    part = jnp.sum(lax.all_to_all(part, PLANE, 0, 0, tiled=True), axis=0)
    for step in (1, 2, 7):
        part = part + lax.ppermute(part, "z", [(i, i ^ step) for i in range(8)])
    ga = gather(part[:GROWS], PLANE, 16).reshape(16 * GROWS, NB)
    gb = swap(ga)
    out = transform(scal, ga, gb, part[GROWS : GROWS + 8], xa, xb, mean)
    return lax.all_to_all(out, CHIPS, 0, 1).reshape(64, CELLS)


def solution(mesh):
    names = ("yh", "x", "core", "z", "yl")
    split = Mesh(mesh.devices.reshape(2, 4, 2, 8, 2), names)
    mem, sp = names[:3], names[3:]
    return jax.shard_map(
        per_device,
        mesh=split,
        in_specs=(P(mem, sp), P(sp), P(sp), P(sp)),
        out_specs=P(mem, sp),
        check_vma=False,
    )
```

```python
import math

import jax
import jax.numpy as jnp
from jax import lax
from jax.experimental import pallas as pl
from jax.experimental.pallas import tpu as pltpu
from jax.sharding import Mesh, PartitionSpec as P

F32 = jnp.float32
BF = jnp.bfloat16
N = 1024
CELLS = 4096
OBS = 8192
NB = 128
SB = 8
NK = N // NB
PART = CELLS // NK
PART_HI = PART // NB
GROWS = 144
VMEM = pl.BlockSpec(memory_space=pltpu.VMEM)
SMEM = pl.BlockSpec(memory_space=pltpu.SMEM)
NTDOT = (((1,), (1,)), ((), ()))


def params(mib):
    return pltpu.CompilerParams(vmem_limit_bytes=mib * 2**20)


def split3(x):
    h = x.astype(BF)
    r = x - h.astype(F32)
    m = r.astype(BF)
    return h, m, (r - m.astype(F32)).astype(BF)


def at(i, size):
    return pl.ds(pl.multiple_of(i * size, size), size)


def obs_kernel(scal, off_ref, data_ref, sigma_ref, out_ref, lhs, oh):
    first = (scal[0] * 4 + scal[1]) * PART_HI
    row = lax.broadcasted_iota(jnp.int32, (8, NB), 0)
    hi_iota = (row & 3) + first
    lower = row < 4
    lo_iota = lax.broadcasted_iota(jnp.int32, (NB, NB), 0)
    for r in range(OBS // NB):
        off = off_ref[r : r + 1, :]
        sigma = sigma_ref[r : r + 1, :]
        w = 1.0 / (sigma * sigma)
        s = data_ref[r : r + 1, :] * w
        mask = lax.shift_right_logical(off, 7) == hi_iota
        cols = slice(r * NB, (r + 1) * NB)
        v = [x.astype(F32) for x in split3(w) + split3(s)]
        blocks = [jnp.where(mask, jnp.where(lower, v[2 * i], v[2 * i + 1]), 0.0) for i in range(3)]
        lhs[:, cols] = jnp.concatenate(blocks + [jnp.zeros((8, NB), F32)], axis=0).astype(BF)
        oh[:, cols] = jnp.where((off & 127) == lo_iota, 1.0, 0.0).astype(BF)
    t = lax.dot_general(lhs[...], oh[...], NTDOT, preferred_element_type=F32)
    w = t[0:4] + t[4:8] + t[8:12]
    s = t[12:16] + t[16:20] + t[20:24]
    out_ref[...] = jnp.zeros_like(out_ref)
    for h in range(PART_HI):
        out_ref[0:1, h * NB : (h + 1) * NB] = w[h : h + 1]
        out_ref[1:2, h * NB : (h + 1) * NB] = s[h : h + 1]


def obs_sums(scal, off, data, sigma):
    shape = (OBS // NB, NB)
    return pl.pallas_call(
        obs_kernel,
        out_shape=jax.ShapeDtypeStruct((8, PART), F32),
        in_specs=[SMEM, VMEM, VMEM, VMEM],
        out_specs=VMEM,
        scratch_shapes=[pltpu.VMEM((32, OBS), BF), pltpu.VMEM((NB, OBS), BF)],
        compiler_params=params(24),
        cost_estimate=pl.CostEstimate(flops=2 * 32 * NB * OBS, bytes_accessed=200000, transcendentals=0),
        name="obs_sums",
    )(scal, off.reshape(shape), data.reshape(shape), sigma.reshape(shape))


def blocks_of(core):
    return [(4 * core + i, d) for d in range(4) for i in range(4)] + [(2 * core + i, 4) for i in range(2)]


def gram_kernel(scal, ws_ref, xa, xb, out_ref, mean_ref, b):
    core = scal[2]
    total = jnp.zeros((1, PART), F32)
    for i in range(NK):
        total = total + jnp.sum(xa[i].astype(F32), axis=0, keepdims=True) + jnp.sum(xb[i].astype(F32), axis=0, keepdims=True)
    mean = total * (1.0 / N)
    mean_ref[...] = jnp.broadcast_to(mean, (8, PART))
    w = ws_ref[0:1, :]
    root = jnp.sqrt(w)
    for i in range(NK):
        b[at(2 * i + core, 64), :] = ((xa[i].astype(F32) - mean) * root).astype(BF)
        b[at(2 * i + 1 - core, 64), :] = ((xb[i].astype(F32) - mean) * root).astype(BF)
    d = jnp.where(w > 0.0, (ws_ref[1:2, :] - mean * w) * lax.rsqrt(jnp.where(w > 0.0, w, 1.0)), 0.0)
    d = jnp.concatenate([x.astype(F32) for x in split3(d)] + [jnp.zeros((13, PART), F32)], axis=0).astype(BF)
    drive = lax.dot_general(d, b[...], NTDOT, preferred_element_type=F32)
    drive = jnp.sum(drive, axis=0, keepdims=True)
    drive = jnp.concatenate([drive[:, i * NB : (i + 1) * NB] for i in range(NK)], axis=0)
    for t in range(16):
        out_ref[t, GROWS:, :] = drive
    for n, (i, d) in enumerate(blocks_of(0)):
        i = i + core * (4 if d < 4 else 2)
        g = lax.dot_general(b[at(i, NB), :], b[at((i + d) % NK, NB), :], NTDOT, preferred_element_type=F32)
        row = 0
        while row < NB:
            t, r = divmod(n * NB + row, GROWS)
            size = min(NB - row, GROWS - r)
            out_ref[t, r : r + size, :] = g[row : row + size]
            row += size


def gram_part(scal, ws, xa, xb):
    return pl.pallas_call(
        gram_kernel,
        out_shape=(jax.ShapeDtypeStruct((16, GROWS + 8, NB), F32), jax.ShapeDtypeStruct((8, PART), F32)),
        in_specs=[SMEM] + [VMEM] * 3,
        out_specs=(VMEM, VMEM),
        scratch_shapes=[pltpu.VMEM((N, PART), BF)],
        compiler_params=params(32),
        cost_estimate=pl.CostEstimate(flops=2 * NB * NB * 18 * PART, bytes_accessed=3 * 2**20, transcendentals=0),
        name="gram_part",
    )(scal, ws, xa, xb)


def diag_inverse(dz, vout, eb, thunks):
    steps = NB // SB
    done = 0
    now = dz[0:SB, 0:NB]
    for j in range(steps):
        r0 = j * SB
        rs = [jnp.broadcast_to(dz[r0 + p : r0 + p + 1, 0:NB], (SB, NB)) for p in range(SB)]
        rw = [jnp.broadcast_to(dz[r0 + p : r0 + p + 1, NB : 2 * NB], (SB, NB)) for p in range(SB)]
        for p in range(SB):
            eb[p] = jnp.broadcast_to(now[:, r0 + p : r0 + p + 1], (SB, NB))
        e = [[jnp.broadcast_to(eb[p, q : q + 1, :], (SB, NB)) for p in range(q + 1)] for q in range(SB)]
        c = {}
        for g in range(j + 1, steps):
            below = dz[g * SB : (g + 1) * SB, 0:NB]
            c[g] = [jnp.broadcast_to(below[:, r0 + p : r0 + p + 1], (SB, NB)) for p in range(SB)]

        def subtract(g, s, w):
            ds = dz[g * SB : (g + 1) * SB, 0:NB]
            dw = dz[g * SB : (g + 1) * SB, NB : 2 * NB]
            for p in range(SB):
                ds = ds - c[g][p] * s[p]
                dw = dw - c[g][p] * w[p]
            dz[g * SB : (g + 1) * SB, 0:NB] = ds
            dz[g * SB : (g + 1) * SB, NB : 2 * NB] = dw
            return ds

        following = range(j + 1, min(j + 2, steps))
        f, r = [], []
        for p in range(SB):
            r.append(lax.rsqrt(e[p][p]))
            rs[p] = rs[p] * r[p]
            rw[p] = rw[p] * r[p]
            f.append({q: e[q][p] * r[p] for q in range(p + 1, SB)})
            for q in range(p + 1, SB):
                for s in range(p + 1, q + 1):
                    e[q][s] = e[q][s] - f[p][q] * f[p][s]
            for q in range(p + 1, SB):
                rs[q] = rs[q] - f[p][q] * rs[p]
                rw[q] = rw[q] - f[p][q] * rw[p]
            for g in following:
                c[g][p] = c[g][p] * r[p]
                for q in range(p + 1, SB):
                    c[g][q] = c[g][q] - f[p][q] * c[g][p]
        for p in range(SB):
            vout[r0 + p : r0 + p + 1, :] = rw[p][0:1, :]
        for g in following:
            now = subtract(g, rs, rw)
        if j + 2 < steps:
            for v in (rs, rw):
                for p in range(SB - 1, -1, -1):
                    for q in range(p + 1, SB):
                        v[p] = v[p] - f[p][q] * v[q]
                    v[p] = v[p] * r[p]
            for g in range(j + 2, steps):
                subtract(g, rs, rw)
        while done < len(thunks) * (j + 1) // steps:
            thunks[done]()
            done += 1


def blk(i, n=1):
    return slice(i * NB, (i + n) * NB)


def inverse_factor(z, dz, vb, eb, ab, lhs, rhs):
    rows = lax.broadcasted_iota(jnp.int32, (NB, NB), 0)
    eye = jnp.where(rows == lax.broadcasted_iota(jnp.int32, (NB, NB), 1), 1.0, 0.0)

    def put(side, j, n, r):
        h, m, l = split3(r)
        for i, x in enumerate([h, m, h, l, h, m]):
            rhs[side, blk(i), blk(j, n)] = x

    def put_inverse(side, j, n, r):
        h, m, _ = split3(r)
        for i, x in enumerate([h, m, h]):
            rhs[side, blk(i), blk(j, n)] = x

    def own(k):
        v = vb[k % 2]
        z[blk(k), blk(k)] = v
        put_inverse(k % 2, k, 1, v)

    def row(k, j, n):
        side = k % 2
        h, m, l = split3(z[blk(k), blk(j, n)])
        if j < k:
            r = jnp.dot(ab[side, :, blk(0, 3)], jnp.concatenate([h, m, h], axis=0), preferred_element_type=F32)
            put_inverse(side, j, n, r)
            z[blk(k), blk(j, n)] = r
            return
        r = jnp.dot(ab[side], jnp.concatenate([h, m, h, l, h, m], axis=0), preferred_element_type=F32)
        put(side, j, n, r)
        for q in range(n):
            x = split3(r[:, blk(q)].T)
            for i, t in enumerate([0, 0, 1, 0, 2, 1]):
                lhs[side, blk(j + q), blk(i)] = x[t]

    def reduce(side, i, m, j, n, terms=6):
        cut = blk(0, terms)
        prod = jnp.dot(lhs[side, blk(i, m), cut], rhs[side, cut, blk(j, n)], preferred_element_type=F32)
        z[blk(i, m), blk(j, n)] = z[blk(i, m), blk(j, n)] - prod

    pending = []

    def later(f, *args):
        pending.append(lambda: f(*args))

    for k in range(NK):
        side = k % 2
        dz[:, 0:NB] = z[blk(k), blk(k)]
        dz[:, NB : 2 * NB] = eye
        diag_inverse(dz, vb.at[side], eb.at[side], pending)
        pending.clear()
        h, m, l = split3(vb[side])
        for i, x in enumerate([h, h, m, h, l, m]):
            ab[side, :, blk(i)] = x
        later(own, k)
        if k + 1 < NK:
            row(k, k + 1, 1)
            reduce(side, k + 1, 1, k + 1, 1)
        for j in range(0, k, 2):
            later(row, k, j, min(2, k - j))
        for j in range(k + 2, NK, 2):
            later(row, k, j, min(2, NK - j))
        if k + 1 < NK:
            for j in range(0, k + 1, 2):
                later(reduce, side, k + 1, 1, j, min(2, k + 1 - j), 3)
            for j in range(k + 2, NK, 2):
                later(reduce, side, k + 1, 1, j, min(2, NK - j))
        for j in range(0, k + 1, 2):
            for i in range(k + 2, NK, 3):
                later(reduce, side, i, min(3, NK - i), j, min(2, k + 1 - j), 3)
        for j in range(k + 2, NK, 2):
            n = min(2, NK - j)
            for i in range(k + 2, j + 1, 3):
                later(reduce, side, i, min(3, j + 1 - i), j, n)
            if n == 2:
                later(reduce, side, j + 1, 1, j + 1, 1)
    for f in pending:
        f()


def transform_kernel(scal, ga, gb, drive_ref, xa, xb, mean_ref, out_ref, z, dz, vb, eb, ab, lhs, rhs, t, x):
    core = scal[2]
    rows = lax.broadcasted_iota(jnp.int32, (NB, NB), 0)
    ridge = jnp.where(rows == lax.broadcasted_iota(jnp.int32, (NB, NB), 1), N - 1.0, 0.0)
    zero_core = (rows * 0 + core) == 0
    for i in range(1, NK):
        z[blk(i), 0 : i * NB] = jnp.zeros((NB, i * NB), F32)
    for c in range(2):
        for n, (i, d) in enumerate(blocks_of(c)):
            j = i + d
            a = ga[blk(n), :]
            b = gb[blk(n), :]
            g = jnp.where(zero_core, a, b) if c == 0 else jnp.where(zero_core, b, a)
            if d == 0:
                z[blk(i), blk(i)] = g + ridge
            elif j < NK:
                z[blk(i), blk(j)] = g
            else:
                z[blk(j - NK), blk(i)] = g.T
    inverse_factor(z, dz, vb, eb, ab, lhs, rhs)
    drive = jnp.concatenate([drive_ref[i : i + 1, :] for i in range(NK)], axis=1)
    sums = [jnp.zeros((8, NB), F32) for _ in range(NK)]
    for i in range(NK):
        width = (i + 1) * NB
        for h in range(2):
            y = z[i * NB + 64 * h : i * NB + 64 * h + 64, 0:width]
            y = y * jnp.sum(y * drive[:, 0:width], axis=1, keepdims=True)
            for q in range(8):
                for j in range(i + 1):
                    sums[j] = sums[j] + y[q * 8 : (q + 1) * 8, blk(j)]
    weights = jnp.sum(jnp.concatenate(sums, axis=1), axis=0, keepdims=True)
    corr = []
    for i in range(NK):
        own = z[at(2 * i + core, 64), 0 : (i + 1) * NB] * math.sqrt(N - 1)
        if i + 1 < NK:
            own = jnp.concatenate([own, jnp.zeros((64, N - (i + 1) * NB), F32)], axis=1)
        own = (own + weights).astype(BF)
        t[i * 64 : (i + 1) * 64, :] = own
        corr.append(1.0 - jnp.sum(own.astype(F32), axis=1, keepdims=True))
        x[at(2 * i + core, 64), :] = xa[i]
        x[at(2 * i + 1 - core, 64), :] = xb[i]
    for i in range(0, NK, 2):
        y = jnp.dot(t[i * 64 : (i + 2) * 64, :], x[...], preferred_element_type=F32)
        for j in range(2):
            out_ref[i + j] = (y[64 * j : 64 * j + 64] + corr[i + j] * mean_ref[0:1, :]).astype(BF)


def transform(scal, ga, gb, drive, xa, xb, mean):
    return pl.pallas_call(
        transform_kernel,
        out_shape=jax.ShapeDtypeStruct((NK, 64, PART), BF),
        in_specs=[SMEM] + [VMEM] * 6,
        out_specs=VMEM,
        scratch_shapes=[
            pltpu.VMEM((N, N), F32),
            pltpu.VMEM((NB, 2 * NB), F32),
            pltpu.VMEM((2, NB, NB), F32),
            pltpu.VMEM((2, SB, SB, NB), F32),
            pltpu.VMEM((2, NB, 6 * NB), BF),
            pltpu.VMEM((2, N, 6 * NB), BF),
            pltpu.VMEM((2, 6 * NB, N), BF),
            pltpu.VMEM((N // 2, N), BF),
            pltpu.VMEM((N, PART), BF),
        ],
        compiler_params=params(40),
        cost_estimate=pl.CostEstimate(flops=10**10, bytes_accessed=4 * 2**20, transcendentals=0),
        name="transform",
    )(scal, ga, gb, drive, xa, xb, mean)


def swap(x):
    return lax.ppermute(x, "core", [(0, 1), (1, 0)])


CHIPS = ("yh", "x")
PLANE = ("yh", "x", "yl")


def gather(x, axes, size):
    return lax.all_to_all(jnp.broadcast_to(x[None], (size, *x.shape)), axes, 0, 0, tiled=True)


def per_device(background_samples, sensor_cell_offsets, sensor_data, sensor_sigma_list):
    core = lax.axis_index("core")
    scal = jnp.stack([lax.axis_index("yh"), lax.axis_index("x"), core]).astype(jnp.int32)
    xa = lax.all_to_all(background_samples.reshape(64, NK, PART), CHIPS, 1, 0)
    xb = swap(xa)
    ws = obs_sums(scal, sensor_cell_offsets, sensor_data, sensor_sigma_list)
    part, mean = gram_part(scal, ws, xa, xb)
    part = jnp.sum(lax.all_to_all(part, PLANE, 0, 0, tiled=True), axis=0)
    for step in (1, 2, 7):
        part = part + lax.ppermute(part, "z", [(i, i ^ step) for i in range(8)])
    ga = gather(part[:GROWS], PLANE, 16).reshape(16 * GROWS, NB)
    gb = swap(ga)
    out = transform(scal, ga, gb, part[GROWS : GROWS + 8], xa, xb, mean)
    return lax.all_to_all(out, CHIPS, 0, 1).reshape(64, CELLS)


def solution(mesh):
    names = ("yh", "x", "core", "z", "yl")
    split = Mesh(mesh.devices.reshape(2, 4, 2, 8, 2), names)
    mem, sp = names[:3], names[3:]
    return jax.shard_map(
        per_device,
        mesh=split,
        in_specs=(P(mem, sp), P(sp), P(sp), P(sp)),
        out_specs=P(mem, sp),
        check_vma=False,
    )
```
